256 devices in a mesh: pts: 64 (over z, y, core), rep: 4 (over x).
Axes of the slice: x: 4, y: 4, z: 8, core: 2. Of those that a mesh axis runs over, the one named last changes fastest.
Arguments:
- feats: bfloat16 [4, 131072, 64], P('rep', 'pts'), may hold values from -6 to 6
- dest_first: int32 [4, 131072], P('rep', 'pts'), may hold values from 0 to 131071, as said below
- pool_ids: int32 [4, 131072], P('rep', 'pts'), may hold values from 0 to 511, as said below
- dest_second: int32 [4, 32768], P('rep', 'pts'), may hold values from 0 to 32767, as said below
- cotangent: bfloat16 [4, 32768, 128], P('rep', 'pts'), may hold values from -6 to 6
- inlet_first: bfloat16 [64, 192], replicated, may hold values from -0.75 to 0.75
- outlet_first: bfloat16 [64, 64], replicated, may hold values from -0.75 to 0.75
- widen_first: bfloat16 [64, 256], replicated, may hold values from -0.75 to 0.75
- narrow_first: bfloat16 [256, 64], replicated, may hold values from -0.375 to 0.375
- pool_weight: bfloat16 [64, 128], replicated, may hold values from -0.75 to 0.75
- inlet_second: bfloat16 [128, 384], replicated, may hold values from -0.5 to 0.5
- outlet_second: bfloat16 [128, 128], replicated, may hold values from -0.5 to 0.5
- widen_second: bfloat16 [128, 512], replicated, may hold values from -0.5 to 0.5
- narrow_second: bfloat16 [512, 128], replicated, may hold values from -0.25 to 0.25
Outputs:
- second_out: bfloat16 [4, 32768, 128], P('rep', 'pts')
- feats_grad: bfloat16 [4, 131072, 64], P('rep', 'pts')
- grad_inlet_first: float32 [64, 192], replicated
- grad_outlet_first: float32 [64, 64], replicated
- grad_widen_first: float32 [64, 256], replicated
- grad_narrow_first: float32 [256, 64], replicated
- grad_pool_weight: float32 [64, 128], replicated
- grad_inlet_second: float32 [128, 384], replicated
- grad_outlet_second: float32 [128, 128], replicated
- grad_widen_second: float32 [128, 512], replicated
- grad_narrow_second: float32 [512, 128], replicated
The draws below stay inside these ranges and needn't reach their ends.
Inputs may be any that keep to these rules, and one draw needn't show every extreme that they name: For each scan a permutation of the positions; the points of one device (aligned blocks of 2048) go to device dest_first // 2048 with at most 64 of them to any one device, and exactly 64 to some devices. `pool_ids`: within each aligned block of 2048 rows the values never fall, every value from 0 to 511 occurs on 1 to 7 consecutive rows, and some value on exactly 7. For each scan a permutation of the positions; the pooled points of one device (aligned blocks of 512) go to device dest_second // 512 with at most 16 of them to any one device, and exactly 16 to some devices.
All inputs are finite; a program needn't handle non-finite values.
Results may differ from the reference program's by a relative error of at most 0.028.
Values may be sent and summed in bfloat16 or wider, within the bound.
A program may use at most 128 MiB of HBM per device.

```python
import math
import jax
import jax.numpy as jnp
from jax import lax

WIDTH_ONE = 64
WIDTH_TWO = 128
HEAD_SIZE = 16
PATCH = 512
ROWS = 2048
COARSE = 512
SCANS = 4
POINTS = 131072
CPOINTS = 32768


def routed_order(key, devices, per_device):
    base = per_device // devices
    quarter = devices // 4
    kind_key, send_key, land_key = jax.random.split(key, 3)
    kinds = jax.random.permutation(kind_key, devices)
    pattern = jnp.where(kinds < quarter, 2 * base, jnp.where(kinds < 2 * quarter, 0, base)).astype(jnp.int32)
    index = jnp.arange(devices, dtype=jnp.int32)
    counts = pattern[(index[None, :] - index[:, None]) % devices]
    ends = jnp.cumsum(counts, axis=1)
    firsts = ends - counts
    inbound = jnp.cumsum(counts, axis=0) - counts
    ranks = jax.vmap(lambda single: jax.random.permutation(single, per_device))(jax.random.split(send_key, devices)).astype(jnp.int32)
    arrange = jax.vmap(lambda single: jax.random.permutation(single, per_device))(jax.random.split(land_key, devices)).astype(jnp.int32)
    target = jax.vmap(lambda bounds, query: jnp.searchsorted(bounds, query, side='right'))(ends, ranks).astype(jnp.int32)
    within = ranks - jnp.take_along_axis(firsts, target, axis=1)
    before = inbound[target, index[:, None]]
    landing = arrange[target, before + within]
    return (target * per_device + landing).astype(jnp.int32)


def segment_block(key, coarse_count, per_device):
    pair_key, order_key = jax.random.split(key)
    shifts = jax.random.randint(pair_key, (coarse_count // 2,), 0, 4).astype(jnp.int32).at[0].set(3)
    sizes = jnp.concatenate([4 + shifts, 4 - shifts])
    sizes = sizes[jax.random.permutation(order_key, coarse_count)]
    ends = jnp.cumsum(sizes)
    marks = jnp.zeros((per_device,), jnp.int32).at[ends[:-1]].set(1)
    return jnp.cumsum(marks).astype(jnp.int32)


def draw_dest_first(key, part):
    key = jax.random.fold_in(key, 11)
    keys = jax.random.split(key, SCANS)
    return jax.vmap(lambda single: routed_order(single, POINTS // ROWS, ROWS).reshape(POINTS))(keys)


def draw_dest_second(key, part):
    key = jax.random.fold_in(key, 12)
    keys = jax.random.split(key, SCANS)
    return jax.vmap(lambda single: routed_order(single, CPOINTS // COARSE, COARSE).reshape(CPOINTS))(keys)


def draw_pool_ids(key, part):
    key = jax.random.fold_in(key, 13)
    keys = jax.random.split(key, SCANS * (POINTS // ROWS))
    ident = jax.vmap(lambda single: segment_block(single, COARSE, ROWS))(keys)
    return ident.reshape(SCANS, POINTS)


def block_levels(own_key, shape, shards, least, top_value):
    gain, own = 1.0, jax.random.fold_in(own_key, 6)
    for dim, shards_of in shards:
        steps = jnp.exp(jax.random.uniform(jax.random.fold_in(own, dim), (shards_of,), jnp.float32, least / len(shards), top_value / len(shards)))
        gain = gain * jnp.repeat(steps, shape[dim] // shards_of).reshape([-1 if axis == dim else 1 for axis in range(len(shape))])
    return gain


def normal_values(rng, extent, deviation, bound, cuts=(), held_as=jnp.bfloat16):
    drawn = jax.random.normal(rng, extent, jnp.float32) * deviation
    if len(cuts) > 0:
        drawn = block_levels(rng, extent, cuts, -0.22, 0.18) * drawn
    return jnp.clip(drawn, min=-bound, max=bound).astype(held_as)


def setup_inputs(seed: int = 0) -> dict:
    arg_keys = jax.random.split(jax.random.key(seed), 15)
    feats = normal_values(arg_keys[0], (SCANS, POINTS, WIDTH_ONE), 1.0, 6.0, ((0, 4), (1, 64)))
    dest_first = draw_dest_first(jax.random.fold_in(arg_keys[14], 71), 0)
    pool_ids = draw_pool_ids(jax.random.fold_in(arg_keys[14], 71), 0)
    dest_second = draw_dest_second(jax.random.fold_in(arg_keys[14], 71), 0)
    cotangent = normal_values(arg_keys[4], (SCANS, CPOINTS, WIDTH_TWO), 1.0, 6.0, ((0, 4), (1, 64)))
    inlet_first = normal_values(arg_keys[5], (WIDTH_ONE, 3 * WIDTH_ONE), WIDTH_ONE ** -0.5, 0.75)
    outlet_first = normal_values(arg_keys[6], (WIDTH_ONE, WIDTH_ONE), WIDTH_ONE ** -0.5, 0.75)
    widen_first = normal_values(arg_keys[7], (WIDTH_ONE, 4 * WIDTH_ONE), WIDTH_ONE ** -0.5, 0.75)
    narrow_first = normal_values(arg_keys[8], (4 * WIDTH_ONE, WIDTH_ONE), (4 * WIDTH_ONE) ** -0.5, 0.375)
    pool_weight = normal_values(arg_keys[9], (WIDTH_ONE, WIDTH_TWO), WIDTH_ONE ** -0.5, 0.75)
    inlet_second = normal_values(arg_keys[10], (WIDTH_TWO, 3 * WIDTH_TWO), WIDTH_TWO ** -0.5, 0.5)
    outlet_second = normal_values(arg_keys[11], (WIDTH_TWO, WIDTH_TWO), WIDTH_TWO ** -0.5, 0.5)
    widen_second = normal_values(arg_keys[12], (WIDTH_TWO, 4 * WIDTH_TWO), WIDTH_TWO ** -0.5, 0.5)
    narrow_second = normal_values(arg_keys[13], (4 * WIDTH_TWO, WIDTH_TWO), (4 * WIDTH_TWO) ** -0.5, 0.25)
    return {"feats": feats, "dest_first": dest_first, "pool_ids": pool_ids, "dest_second": dest_second, "cotangent": cotangent, "inlet_first": inlet_first, "outlet_first": outlet_first, "widen_first": widen_first, "narrow_first": narrow_first, "pool_weight": pool_weight, "inlet_second": inlet_second, "outlet_second": outlet_second, "widen_second": widen_second, "narrow_second": narrow_second}


def layer_norm(values):
    centred = values - lax.optimization_barrier(jnp.mean(values, axis=-1, keepdims=True))
    return centred * lax.rsqrt(lax.optimization_barrier(jnp.mean(centred * centred, axis=-1, keepdims=True)) + 1e-05)

def zero_taps(row_count, feature_width):
    return (jnp.zeros((row_count, 3 * feature_width), jnp.float32), jnp.zeros((row_count, feature_width), jnp.float32), jnp.zeros((row_count, 4 * feature_width), jnp.float32), jnp.zeros((row_count, feature_width), jnp.float32))

def block(inputs, weights, tap_zeros):
    inlet_weight, outlet, widen_weight, narrow = weights
    row_count, feature_width = inputs.shape
    head_count = feature_width // HEAD_SIZE
    initial = inputs.astype(jnp.float32)
    normed = layer_norm(initial).astype(jnp.bfloat16)
    mixed_rows = (jnp.dot(normed, inlet_weight, preferred_element_type=jnp.float32) + tap_zeros[0]).astype(jnp.bfloat16)
    parted = mixed_rows.reshape(row_count // PATCH, PATCH, 3, head_count, HEAD_SIZE)
    scores = jnp.einsum('bqhd,bkhd->bhqk', parted[:, :, 0].astype(jnp.float32), parted[:, :, 1].astype(jnp.float32)) * HEAD_SIZE ** (-0.5)
    softmax_weights = jax.nn.softmax(scores, axis=-1).astype(jnp.bfloat16)
    attended = jnp.einsum('bhqk,bkhd->bqhd', softmax_weights.astype(jnp.float32), parted[:, :, 2].astype(jnp.float32))
    attended = attended.astype(jnp.bfloat16).reshape(row_count, feature_width)
    middle = initial + jnp.dot(attended, outlet, preferred_element_type=jnp.float32) + tap_zeros[1]
    second = layer_norm(middle).astype(jnp.bfloat16)
    hidden = jax.nn.gelu(jnp.dot(second, widen_weight, preferred_element_type=jnp.float32) + tap_zeros[2], approximate=False).astype(jnp.bfloat16)
    result = (middle + jnp.dot(hidden, narrow, preferred_element_type=jnp.float32) + tap_zeros[3]).astype(jnp.bfloat16)
    return (result, (normed, attended, second, hidden))

def weight_grad(inputs, gradient):
    return jnp.dot(inputs.T, gradient.astype(jnp.bfloat16), preferred_element_type=jnp.float32)

def run_block(inputs, weights):
    tap_zeros = zero_taps(inputs.shape[0], inputs.shape[1])
    result, pullback, saved = jax.vjp(lambda given, taps_in: block(given, weights, taps_in), inputs, tap_zeros, has_aux=True)

    def finish(gradient):
        grad_rows, grad_taps = pullback(gradient)
        return (grad_rows, tuple((weight_grad(saved[index], grad_taps[index]) for index in range(4))))
    return (result, finish)

def pool_rows(inputs, ident, coarse_count):
    member = ident[None, :] == jnp.arange(coarse_count, dtype=jnp.int32)[:, None]
    sums = jnp.dot(member.astype(jnp.bfloat16), inputs, preferred_element_type=jnp.float32)
    sizes = lax.optimization_barrier(jnp.sum(member.astype(jnp.float32), axis=1, keepdims=True))
    return (sums / sizes).astype(jnp.bfloat16)

def project(pooled, weight, tap_zero):
    return (jnp.dot(pooled, weight, preferred_element_type=jnp.float32) + tap_zero).astype(jnp.bfloat16)

def run_project(pooled, weight):
    tap_zero = jnp.zeros((pooled.shape[0], weight.shape[1]), jnp.float32)
    result, pullback = jax.vjp(lambda given, tap_in: project(given, weight, tap_in), pooled, tap_zero)

    def finish(gradient):
        grad_pooled, grad_tap = pullback(gradient)
        return (grad_pooled, weight_grad(pooled, grad_tap))
    return (result, finish)

def place_rows(values, targets):
    return jnp.zeros_like(values).at[targets].set(values)

def reference(feats, dest_first, pool_ids, dest_second, cotangent, inlet_first, outlet_first, widen_first, narrow_first, pool_weight, inlet_second, outlet_second, widen_second, narrow_second):
    first = (inlet_first, outlet_first, widen_first, narrow_first)
    second = (inlet_second, outlet_second, widen_second, narrow_second)
    scans, points, width_one = feats.shape
    width_two = pool_weight.shape[1]
    blocks = scans * (points // ROWS)
    serial_one = jax.vmap(place_rows)(feats, dest_first).reshape(blocks, ROWS, width_one)
    ident = pool_ids.reshape(blocks, ROWS)

    def section_one(pair):
        fine_out = block(pair[0], first, zero_taps(ROWS, width_one))[0]
        pooled = pool_rows(fine_out, pair[1], COARSE)
        return project(pooled, pool_weight, jnp.zeros((COARSE, width_two), jnp.float32))
    coarse_in = lax.map(section_one, (serial_one, ident)).reshape(scans, CPOINTS, width_two)
    serial_two = jax.vmap(place_rows)(coarse_in, dest_second).reshape(blocks, COARSE, width_two)
    cot_blocks = cotangent.reshape(blocks, COARSE, width_two)

    def section_two(carry, pair):
        second_block, finish = run_block(pair[0], second)
        grad_rows, grads = finish(pair[1])
        return (tuple((carry[index] + grads[index] for index in range(4))), (second_block, grad_rows))
    init_two = tuple((jnp.zeros(weight.shape, jnp.float32) for weight in second))
    totals_two, (second_out, grad_serial_two) = lax.scan(section_two, init_two, (serial_two, cot_blocks))
    grad_coarse = jax.vmap(lambda grads, targets: grads[targets])(grad_serial_two.reshape(scans, CPOINTS, width_two), dest_second)
    grad_coarse = grad_coarse.reshape(blocks, COARSE, width_two)

    def section_one_back(carry, triple):
        fine_out, finish_first = run_block(triple[0], first)
        pooled, finish_pool = jax.vjp(lambda given: pool_rows(given, triple[1], COARSE), fine_out)
        unused, finish_proj = run_project(pooled, pool_weight)
        grad_pooled, grad_pool = finish_proj(triple[2])
        grad_fine = finish_pool(grad_pooled)[0]
        grad_rows, grads = finish_first(grad_fine)
        sums = tuple((carry[index] + grads[index] for index in range(4))) + (carry[4] + grad_pool,)
        return (sums, grad_rows)
    init_one = tuple((jnp.zeros(weight.shape, jnp.float32) for weight in first)) + (jnp.zeros(pool_weight.shape, jnp.float32),)
    totals_one, grad_serial_one = lax.scan(section_one_back, init_one, (serial_one, ident, grad_coarse))
    feats_grad = jax.vmap(lambda grads, targets: grads[targets])(grad_serial_one.reshape(scans, points, width_one), dest_first)
    scale = 1.0 / math.sqrt(SCANS * CPOINTS)
    grads = tuple((total * scale for total in totals_one + totals_two))
    return (second_out.reshape(scans, CPOINTS, width_two), feats_grad, grads[0], grads[1], grads[2], grads[3], grads[4], grads[5], grads[6], grads[7], grads[8])
```

```python
import math

import jax
import jax.numpy as jnp
from jax import lax
from jax.experimental import pallas as pl
from jax.experimental.pallas import tpu as pltpu
from jax.sharding import PartitionSpec as P

HEAD_SIZE = 16
PATCH = 512


def shortened(array):

    def short(part):
        return part.astype(jnp.bfloat16) if part.dtype == jnp.float32 else part

    return jax.tree.map(short, array)


def layer_norm(values):
    centred = values - jnp.mean(values, axis=-1, keepdims=True)
    return centred * lax.rsqrt(jnp.mean(centred * centred, axis=-1, keepdims=True) + 1e-05)


def zero_taps(row_count, feature_width):
    return (
        jnp.zeros((row_count, 3 * feature_width), jnp.float32),
        jnp.zeros((row_count, feature_width), jnp.float32),
        jnp.zeros((row_count, 4 * feature_width), jnp.float32),
        jnp.zeros((row_count, feature_width), jnp.float32),
    )


def block(inputs, weights, tap_zeros):
    inlet_weight, outlet, widen_weight, narrow = weights
    row_count, feature_width = inputs.shape
    head_count = feature_width // HEAD_SIZE
    initial = inputs.astype(jnp.float32)
    normed = layer_norm(initial).astype(jnp.bfloat16)
    mixed_rows = (
        jnp.dot(normed, inlet_weight, preferred_element_type=jnp.float32) + tap_zeros[0]
    ).astype(jnp.bfloat16)
    parted = mixed_rows.reshape(row_count // PATCH, PATCH, 3, head_count, HEAD_SIZE)
    scores = jnp.einsum(
        "bqhd,bkhd->bhqk", parted[:, :, 0], parted[:, :, 1], preferred_element_type=jnp.float32
    ) * HEAD_SIZE ** (-0.5)
    softmax_weights = jax.nn.softmax(scores, axis=-1).astype(jnp.bfloat16)
    attended = jnp.einsum(
        "bhqk,bkhd->bqhd", softmax_weights, parted[:, :, 2], preferred_element_type=jnp.float32
    )
    attended = attended.astype(jnp.bfloat16).reshape(row_count, feature_width)
    middle = initial + jnp.dot(attended, outlet, preferred_element_type=jnp.float32) + tap_zeros[1]
    second = layer_norm(middle).astype(jnp.bfloat16)
    hidden = jax.nn.gelu(
        jnp.dot(second, widen_weight, preferred_element_type=jnp.float32) + tap_zeros[2],
        approximate=False,
    ).astype(jnp.bfloat16)
    result = (
        middle + jnp.dot(hidden, narrow, preferred_element_type=jnp.float32) + tap_zeros[3]
    ).astype(jnp.bfloat16)
    return (result, (normed, attended, second, hidden))


def weight_grad(inputs, gradient):
    return lax.dot_general(
        inputs,
        gradient.astype(jnp.bfloat16),
        (((0,), (0,)), ((), ())),
        preferred_element_type=jnp.float32,
    )


def run_block(inputs, weights):
    tap_zeros = zero_taps(inputs.shape[0], inputs.shape[1])
    result, pullback, saved = jax.vjp(
        lambda given, taps_in: block(given, weights, taps_in), inputs, tap_zeros, has_aux=True
    )

    def finish(gradient):
        grad_rows, grad_taps = pullback(gradient)
        return (
            grad_rows,
            tuple((weight_grad(saved[index], grad_taps[index]) for index in range(4))),
        )

    return (result, finish)


def pool_rows(inputs, ident, coarse_count):
    member = ident[None, :] == jnp.arange(coarse_count, dtype=jnp.int32)[:, None]
    sums = jnp.dot(member.astype(jnp.bfloat16), inputs, preferred_element_type=jnp.float32)
    sizes = jnp.sum(member.astype(jnp.float32), axis=1, keepdims=True)
    return (sums / sizes).astype(jnp.bfloat16)


def project(pooled, weight, tap_zero):
    return (jnp.dot(pooled, weight, preferred_element_type=jnp.float32) + tap_zero).astype(
        jnp.bfloat16
    )


def run_project(pooled, weight):
    tap_zero = jnp.zeros((pooled.shape[0], weight.shape[1]), jnp.float32)
    result, pullback = jax.vjp(
        lambda given, tap_in: project(given, weight, tap_in), pooled, tap_zero
    )

    def finish(gradient):
        grad_pooled, grad_tap = pullback(gradient)
        return (grad_pooled, weight_grad(pooled, grad_tap))

    return (result, finish)


def pack_slots(targets, row_count, devices, capacity):
    owner = targets // row_count
    place_index = targets % row_count
    hits = (owner[:, None] == jnp.arange(devices, dtype=jnp.int32)[None, :]).astype(jnp.int32)
    rank = jnp.sum(hits * (jnp.cumsum(hits, axis=0) - 1), axis=1)
    slot_index = owner * capacity + rank
    landing = jnp.full((devices * capacity,), row_count, jnp.int32).at[slot_index].set(place_index)
    return (slot_index, landing.reshape(devices, capacity))


def fill_slots(inputs, slot_index, devices, capacity):
    buffer = (
        jnp.zeros((devices * capacity, inputs.shape[1]), inputs.dtype).at[slot_index].set(inputs)
    )
    return buffer.reshape(devices, capacity, inputs.shape[1])


def land_rows(arrived, landing, row_count):
    feature_width = arrived.shape[2]
    placed = (
        jnp.zeros((row_count + 1, feature_width), arrived.dtype)
        .at[landing.reshape(-1)]
        .set(arrived.reshape(-1, feature_width))
    )
    return placed[:row_count]


def take_rows(gradient, landing, devices, capacity):
    feature_width = gradient.shape[1]
    padded = jnp.concatenate([gradient, jnp.zeros((1, feature_width), gradient.dtype)], axis=0)
    return padded[landing.reshape(-1)].reshape(devices, capacity, feature_width)


def pick_rows(returned, slot_index):
    return returned.reshape(-1, returned.shape[2])[slot_index]


NEAR, FAR = 8, 32


def add_kernel(scale, grads_ref, out_ref, half, near, middle, far, chunk, whole, near_out, sems):
    me, rep = lax.axis_index("pts"), lax.axis_index("rep")
    place, core = me // 2, me % 2
    mine = core * 4 + rep
    barrier = pltpu.get_barrier_semaphore()

    def near_device(step):
        other = (mine + step) % NEAR
        return other, {"pts": place * 2 + other // 4, "rep": other % 4}

    def far_device(step):
        other = (place + step) % FAR
        return other, {"pts": other * 2 + core}

    def greet_near(step, carry):
        pl.semaphore_signal(barrier, device_id=near_device(step)[1], device_id_type=pl.DeviceIdType.MESH)
        return carry

    def greet_far(step, carry):
        pl.semaphore_signal(barrier, device_id=far_device(step)[1], device_id_type=pl.DeviceIdType.MESH)
        return carry

    lax.fori_loop(1, NEAR, greet_near, 0)
    lax.fori_loop(1, FAR, greet_far, 0)
    half[...] = grads_ref[...].astype(jnp.bfloat16)
    pl.semaphore_wait(barrier, NEAR + FAR - 2)

    def send_near(step, carry):
        other, device = near_device(step)
        pltpu.make_async_remote_copy(
            half.at[other], near.at[mine], sems.at[0], sems.at[1], device_id=device,
            device_id_type=pl.DeviceIdType.MESH,
        ).start()
        return carry

    lax.fori_loop(1, NEAR, send_near, 0)
    near[mine] = half[mine]
    batch = pltpu.make_async_remote_copy(
        half.at[pl.ds(0, NEAR - 1)], near.at[pl.ds(0, NEAR - 1)], sems.at[0], sems.at[1],
        device_id={"pts": me}, device_id_type=pl.DeviceIdType.MESH,
    )
    batch.wait_recv()
    total = near[0].astype(jnp.float32)
    for index in range(1, NEAR):
        total = total + near[index].astype(jnp.float32)
    middle[...] = total.reshape(FAR, 8, 128)

    def send_far(step, carry):
        other, device = far_device(step)
        pltpu.make_async_remote_copy(
            middle.at[other], far.at[place], sems.at[2], sems.at[3], device_id=device,
            device_id_type=pl.DeviceIdType.MESH,
        ).start()
        return carry

    lax.fori_loop(1, FAR, send_far, 0)
    far[place] = middle[place]
    batch_far = pltpu.make_async_remote_copy(
        middle.at[pl.ds(0, FAR - 1)], far.at[pl.ds(0, FAR - 1)], sems.at[2], sems.at[3],
        device_id={"pts": me}, device_id_type=pl.DeviceIdType.MESH,
    )
    batch_far.wait_recv()
    chunk[...] = jnp.sum(far[...], axis=0) * scale

    def spread_far(step, carry):
        device = far_device(step)[1]
        pltpu.make_async_remote_copy(
            chunk, whole.at[place], sems.at[4], sems.at[5], device_id=device,
            device_id_type=pl.DeviceIdType.MESH,
        ).start()
        return carry

    lax.fori_loop(1, FAR, spread_far, 0)
    whole[place] = chunk[...]
    batch_whole = pltpu.make_async_remote_copy(
        whole.at[pl.ds(0, FAR - 1)], whole.at[pl.ds(0, FAR - 1)], sems.at[4], sems.at[5],
        device_id={"pts": me}, device_id_type=pl.DeviceIdType.MESH,
    )
    batch_whole.wait_recv()
    near_out[...] = whole[...].reshape(256, 128).astype(jnp.bfloat16)

    def spread_near(step, carry):
        device = near_device(step)[1]
        pltpu.make_async_remote_copy(
            near_out, out_ref.at[mine], sems.at[6], sems.at[7], device_id=device,
            device_id_type=pl.DeviceIdType.MESH,
        ).start()
        return carry

    lax.fori_loop(1, NEAR, spread_near, 0)
    out_ref[mine] = near_out[...]
    batch_out = pltpu.make_async_remote_copy(
        out_ref.at[pl.ds(0, NEAR - 1)], out_ref.at[pl.ds(0, NEAR - 1)], sems.at[6], sems.at[7],
        device_id={"pts": me}, device_id_type=pl.DeviceIdType.MESH,
    )
    batch_out.wait_recv()
    batch.wait_send()
    batch_far.wait_send()
    batch_whole.wait_send()
    batch_out.wait_send()


def all_reduce(packed, scale):
    return pl.pallas_call(
        lambda *refs: add_kernel(scale, *refs),
        out_shape=jax.ShapeDtypeStruct((NEAR, 256, 128), jnp.bfloat16),
        in_specs=[pl.BlockSpec(memory_space=pltpu.VMEM)],
        out_specs=pl.BlockSpec(memory_space=pltpu.VMEM),
        scratch_shapes=[
            pltpu.VMEM((NEAR, 256, 128), jnp.bfloat16),
            pltpu.VMEM((NEAR, 256, 128), jnp.bfloat16),
            pltpu.VMEM((FAR, 8, 128), jnp.float32),
            pltpu.VMEM((FAR, 8, 128), jnp.float32),
            pltpu.VMEM((8, 128), jnp.float32),
            pltpu.VMEM((FAR, 8, 128), jnp.float32),
            pltpu.VMEM((256, 128), jnp.bfloat16),
            pltpu.SemaphoreType.DMA((8,)),
        ],
        compiler_params=pltpu.CompilerParams(collective_id=1, has_side_effects=True),
    )(packed)


def lanes(array):
    return [array[:, start : start + 128] for start in range(0, array.shape[1], 128)]


def pack_totals(first, pool, second):
    rows = [jnp.concatenate(first[:2], axis=1)[:, :128], jnp.concatenate(first[:2], axis=1)[:, 128:]]
    rows += lanes(first[2]) + [jnp.concatenate([first[3][:128], first[3][128:]], axis=1), pool]
    rows += lanes(second[0]) + [second[1]] + lanes(second[2]) + [second[3]]
    rows += [jnp.zeros((64, 128), jnp.float32)]
    return jnp.concatenate(rows, axis=0).reshape(NEAR, 256, 128)


def unpack_totals(packed):
    rows = packed.reshape(2048, 128)
    front = jnp.concatenate([rows[:64], rows[64:128]], axis=1)
    widen = jnp.concatenate([rows[128:192], rows[192:256]], axis=1)
    narrow = jnp.concatenate([rows[256:384, :64], rows[256:384, 64:]], axis=0)
    inlet = jnp.concatenate([rows[448 + 128 * i : 576 + 128 * i] for i in range(3)], axis=1)
    wide = jnp.concatenate([rows[960 + 128 * i : 1088 + 128 * i] for i in range(4)], axis=1)
    return (front[:, :192], front[:, 192:], widen, narrow, rows[384:448], inlet, rows[832:960], wide, rows[1472:1984])


def shards(
    feats,
    dest_first,
    pool_ids,
    dest_second,
    cotangent,
    inlet_first,
    outlet_first,
    widen_first,
    narrow_first,
    pool_weight,
    inlet_second,
    outlet_second,
    widen_second,
    narrow_second,
):
    first = (inlet_first, outlet_first, widen_first, narrow_first)
    second = (inlet_second, outlet_second, widen_second, narrow_second)
    devices = lax.axis_size("pts")
    point_rows = feats[0]
    row_count, width_one = point_rows.shape
    coarse_count = dest_second.shape[1]
    capacity_one = 2 * row_count // devices
    capacity_two = 2 * coarse_count // devices
    slot_one, landing_one = pack_slots(dest_first[0], row_count, devices, capacity_one)
    sent_rows, arrived_one = (
        lax.all_to_all(
            fill_slots(point_rows, slot_one, devices, capacity_one),
            "pts",
            split_axis=0,
            concat_axis=0,
            tiled=True,
        ),
        lax.all_to_all(landing_one, "pts", split_axis=0, concat_axis=0, tiled=True),
    )
    serial_one = land_rows(sent_rows, arrived_one, row_count)
    ident = pool_ids[0]
    fine_out, finish_first = run_block(serial_one, first)
    pooled, finish_pool = jax.vjp(lambda given: pool_rows(given, ident, coarse_count), fine_out)
    slot_two, landing_two = pack_slots(dest_second[0], coarse_count, devices, capacity_two)
    coarse_in, finish_proj = run_project(pooled, pool_weight)
    moved, arrived_two = (
        lax.all_to_all(
            shortened(fill_slots(coarse_in, slot_two, devices, capacity_two)),
            "pts",
            split_axis=0,
            concat_axis=0,
            tiled=True,
        ),
        lax.all_to_all(landing_two, "pts", split_axis=0, concat_axis=0, tiled=True),
    )
    serial_two = land_rows(moved, arrived_two, coarse_count)
    second_out, finish_second = run_block(serial_two, second)
    grad_serial_two, grads_second = finish_second(cotangent[0])
    returned = lax.all_to_all(
        shortened(take_rows(grad_serial_two, arrived_two, devices, capacity_two)),
        "pts",
        split_axis=0,
        concat_axis=0,
        tiled=True,
    )
    grad_pooled, grad_pool = finish_proj(pick_rows(returned, slot_two))
    grad_fine = finish_pool(grad_pooled)[0]
    grad_serial_one, grads_first = finish_first(grad_fine)
    back_rows = lax.all_to_all(
        shortened(take_rows(grad_serial_one, arrived_one, devices, capacity_one)),
        "pts",
        split_axis=0,
        concat_axis=0,
        tiled=True,
    )
    feats_grad = pick_rows(back_rows, slot_one)
    packed = pack_totals(grads_first, grad_pool, grads_second)
    scale = 1.0 / math.sqrt(lax.axis_size("rep") * devices * coarse_count)
    scaled = unpack_totals(all_reduce(packed, scale).astype(jnp.float32))
    return (
        second_out[None],
        feats_grad[None],
        scaled[0],
        scaled[1],
        scaled[2],
        scaled[3],
        scaled[4],
        scaled[5],
        scaled[6],
        scaled[7],
        scaled[8],
    )


def solution(mesh):
    return jax.shard_map(
        shards,
        mesh=mesh,
        in_specs=(
            P("rep", "pts", None),
            P("rep", "pts"),
            P("rep", "pts"),
            P("rep", "pts"),
            P("rep", "pts", None),
            P(),
            P(),
            P(),
            P(),
            P(),
            P(),
            P(),
            P(),
            P(),
        ),
        out_specs=(
            P("rep", "pts", None),
            P("rep", "pts", None),
            P(),
            P(),
            P(),
            P(),
            P(),
            P(),
            P(),
            P(),
            P(),
        ),
        check_vma=False,
    )
```

```python
import math

import jax
import jax.numpy as jnp
from jax import lax
from jax.experimental import pallas as pl
from jax.experimental.pallas import tpu as pltpu
from jax.sharding import PartitionSpec as P


HEAD = 16
PATCH = 512
PATCHES = 4
ROWS = 2048
COARSE = 512
PEERS = 64
NEAR, FAR = 8, 32
MESH = pl.DeviceIdType.MESH
SHARPEN = HEAD**-0.5 / math.log(2.0)
f32, bf16, i32 = jnp.float32, jnp.bfloat16, jnp.int32


def dot(left, right):
    return jnp.dot(left, right, preferred_element_type=f32)


def dot_nt(left, right):
    return lax.dot_general(left, right, (((1,), (1,)), ((), ())), preferred_element_type=f32)


def turned(array):
    return array.astype(f32).T.astype(bf16)


def rows_of(count, width):
    return lax.broadcasted_iota(i32, (count, width), 0)


def match(row, count):
    return jnp.where(rows_of(count, row.shape[1]) == row, 1.0, 0.0).astype(bf16)


def norm(values):
    centred = values - jnp.mean(values, axis=0, keepdims=True)
    rate = lax.rsqrt(jnp.mean(centred * centred, axis=0, keepdims=True) + 1e-05)
    return centred * rate, rate


def norm_back(gradient, normed, rate):
    mean = jnp.mean(gradient, axis=0, keepdims=True)
    along = jnp.mean(gradient * normed, axis=0, keepdims=True)
    return rate * (gradient - mean - normed * along)


def gelu_parts(values):
    below = 0.5 + 0.5 * lax.erf(values * math.sqrt(0.5))
    bell = jnp.exp(-0.5 * values * values) * (1.0 / math.sqrt(2.0 * math.pi))
    return values * below, below + values * bell


def only(array, head):
    width = array.shape[1]
    parts = []
    if head > 0:
        parts.append(jnp.zeros((HEAD * head, width), array.dtype))
    parts.append(array[HEAD * head : HEAD * (head + 1)])
    rest = array.shape[0] - HEAD * (head + 1)
    if rest > 0:
        parts.append(jnp.zeros((rest, width), array.dtype))
    return jnp.concatenate(parts, axis=0)


def attend(mixed, width):
    keys = turned(mixed[width : 2 * width])
    ones = jnp.ones((HEAD, PATCH), bf16)
    outs, logs = [], []
    for head in range(width // HEAD):
        scores = dot(keys, only(mixed[:width], head))
        top = jnp.max(scores, axis=0, keepdims=True)
        powers = jnp.exp2((scores - top) * SHARPEN).astype(bf16)
        start = 2 * width + HEAD * head
        sums = dot(jnp.concatenate([mixed[start : start + HEAD], ones], axis=0), powers)
        size = sums[HEAD : HEAD + 1]
        outs.append(sums[:HEAD] / size)
        logs.append(top * SHARPEN + jnp.log2(size))
    return jnp.concatenate(outs, axis=0).astype(bf16), logs


def attend_back(mixed, attended, gradient, logs, width):
    keys = turned(mixed[width : 2 * width])
    values = turned(mixed[2 * width :])
    grad_queries, grad_keys, grad_values = [], [], []
    for head in range(width // HEAD):
        part = slice(HEAD * head, HEAD * (head + 1))
        queries = mixed[part]
        key_rows = mixed[width + HEAD * head : width + HEAD * (head + 1)]
        grad = gradient[part]
        overlap = jnp.sum(
            grad.astype(f32) * attended[part].astype(f32), axis=0, keepdims=True
        )
        scores = dot(keys, only(mixed[:width], head))
        probs = jnp.exp2(scores * SHARPEN - logs[head])
        spread = dot(values, only(gradient, head))
        change = (probs * (spread - overlap)).astype(bf16)
        grad_queries.append(dot(key_rows, change) * HEAD**-0.5)
        grad_keys.append(dot_nt(queries, change) * HEAD**-0.5)
        grad_values.append(dot_nt(grad, probs.astype(bf16)))
    return jnp.concatenate(grad_queries + grad_keys + grad_values, axis=0).astype(bf16)


def block_front(inputs, inlet_t, outlet_t, widen_t, narrow_t):
    width = inputs.shape[0]
    start = inputs.astype(f32)
    normed = norm(start)[0].astype(bf16)
    mixed = dot(inlet_t, normed).astype(bf16)
    attended, logs = attend(mixed, width)
    middle = start + dot(outlet_t, attended)
    second = norm(middle)[0].astype(bf16)
    hidden, slope = gelu_parts(dot(widen_t, second))
    hidden = hidden.astype(bf16)
    result = (middle + dot(narrow_t, hidden)).astype(bf16)
    return result, mixed, attended, logs, hidden, slope.astype(bf16)


def block_back(inputs, mixed, attended, logs, hidden, slope, gradient, weights, outlet_t):
    inlet, outlet, widen, narrow = weights
    width = inputs.shape[0]
    start = inputs.astype(f32)
    normed, rate = norm(start)
    second, rate_two = norm(start + dot(outlet_t, attended))
    grad_narrow = dot_nt(gradient, hidden)
    grad_wide = (dot(narrow, gradient) * slope.astype(f32)).astype(bf16)
    grad_widen = dot_nt(second.astype(bf16), grad_wide)
    grad_middle = gradient.astype(f32) + norm_back(dot(widen, grad_wide), second, rate_two)
    short = grad_middle.astype(bf16)
    grad_outlet = dot_nt(attended, short)
    grad_attended = dot(outlet, short).astype(bf16)
    grad_mixed = attend_back(mixed, attended, grad_attended, logs, width)
    grad_inlet = dot_nt(normed.astype(bf16), grad_mixed)
    grad_inputs = grad_middle + norm_back(dot(inlet, grad_mixed), normed, rate)
    return grad_inputs.astype(bf16), grad_inlet, grad_outlet, grad_widen, grad_narrow


def ranks(owner):
    before_me = jnp.where(rows_of(256, 256) < lax.broadcasted_iota(i32, (256, 256), 1), 1.0, 0.0)
    before_me = before_me.astype(bf16)
    before = jnp.zeros((PEERS, 1), f32)
    found = []
    for start in range(0, owner.shape[1], 256):
        hits = jnp.where(rows_of(PEERS, 256) == owner[:, start : start + 256], 1.0, 0.0)
        count = dot(hits.astype(bf16), before_me) + before
        found.append(jnp.sum(hits * count, axis=0, keepdims=True))
        before = before + jnp.sum(hits, axis=1, keepdims=True)
    return jnp.concatenate(found, axis=1).astype(i32)


def marks(owner, rank, value):
    hits = match(owner, PEERS)
    at = rows_of(128, owner.shape[1]) == rank
    high = jnp.where(at, (value >> 6).astype(f32), 0.0).astype(bf16)
    low = jnp.where(at, (value & 63).astype(f32), 0.0).astype(bf16)
    return dot_nt(hits, high) * 64.0 + dot_nt(hits, low)


def spread_places(table):
    lane = lax.broadcasted_iota(i32, (PEERS, 128), 1)
    apart = table + jnp.where(lane >= 64, 4096.0, 0.0)
    over = jnp.zeros((PEERS, 128), f32)
    for shift in range(1, 64):
        over = jnp.where(apart == pltpu.roll(apart, 128 - shift, 1), 1.0, over)
    high = jnp.floor(table * (1.0 / 64.0))
    low = table - 64.0 * high
    high = high + 64.0 * over
    stack = []
    for part in range(5):
        stack += [high[:, 16 * part : 16 * part + 16], low[:, 16 * part : 16 * part + 16]]
    stack = jnp.concatenate(stack, axis=0).astype(bf16)
    column = lax.broadcasted_iota(i32, (16, 1024), 1)
    spread = dot(stack, jnp.where(column % 16 == rows_of(16, 1024), 1.0, 0.0).astype(bf16))
    own = rows_of(PEERS, 1024) == lax.broadcasted_iota(i32, (PEERS, 1024), 1) // 16
    places, drops = [], []
    for part in range(5):
        high = jnp.sum(jnp.where(own, spread[128 * part : 128 * part + 64], 0.0), axis=0, keepdims=True)
        low = jnp.sum(jnp.where(own, spread[128 * part + 64 : 128 * part + 128], 0.0), axis=0, keepdims=True)
        drops.append(high > 63.5)
        high = jnp.where(high > 63.5, high - 64.0, high)
        places.append((high * 64.0 + low).astype(i32) - 1)
    return places, drops


def last_senders(inside, hits):
    width = hits[0].shape[0]
    count = len(inside[0])
    sender = lax.broadcasted_iota(i32, (1, 1024), 1) // 16
    own = rows_of(PEERS, 1024) == sender
    seen = jnp.zeros((PEERS * count, width), f32)
    for masks, hit in zip(inside, hits):
        wide = [jnp.where(own & mask, 1.0, 0.0) for mask in masks]
        seen += dot_nt(jnp.concatenate(wide, axis=0).astype(bf16), hit)
    index = rows_of(PEERS, width).astype(f32)
    lasts = []
    for part in range(count):
        lasts.append(jnp.max(jnp.where(seen[PEERS * part : PEERS * part + PEERS] > 0.5, index, -1.0), axis=0, keepdims=True))
    lasts = jnp.concatenate(lasts + [jnp.zeros((16 - count, width), f32)], axis=0).astype(bf16)
    found = []
    for masks, hit in zip(inside, hits):
        got = dot(lasts, hit)
        mine = jnp.full((1, 1024), -1.0, f32)
        for part in range(count):
            mine = jnp.where(masks[part], got[part : part + 1], mine)
        found.append(mine == sender.astype(f32))
    return found


def greet_peers(me):
    barrier = pltpu.get_barrier_semaphore()

    def greet(step, carry):
        pl.semaphore_signal(
            barrier, device_id={"pts": (me + step) % PEERS}, device_id_type=MESH
        )
        return carry

    lax.fori_loop(1, PEERS, greet, 0)
    return barrier


def exchange(me, source, target, send_sem, recv_sem):

    def send(step, carry):
        other = (me + step) % PEERS
        pltpu.make_async_remote_copy(
            source.at[other],
            target.at[me],
            send_sem,
            recv_sem,
            device_id={"pts": other},
            device_id_type=MESH,
        ).start()
        return carry

    lax.fori_loop(1, PEERS, send, 0)
    target[me] = source[me]
    return pltpu.make_async_remote_copy(
        source.at[pl.ds(0, PEERS - 1)],
        target.at[pl.ds(0, PEERS - 1)],
        send_sem,
        recv_sem,
        device_id={"pts": me},
        device_id_type=MESH,
    )


def pack_kernel(feats_ref, first_ref, second_ref, rows_ref, places_ref, slot_one_ref, slot_two_ref, send, mark, sems):
    me = lax.axis_index("pts")
    barrier = greet_peers(me)
    first, second = first_ref[...], second_ref[...]
    owner_one, owner_two = first // ROWS, second // COARSE
    rank_one, rank_two = ranks(owner_one), ranks(owner_two)
    found = marks(owner_one, rank_one, first % ROWS + 1)
    found += marks(owner_two, rank_two + 64, second % COARSE + 1)
    mark[:, 0, :] = found
    pl.semaphore_wait(barrier, PEERS - 1)
    marked = exchange(me, mark, places_ref, sems.at[0], sems.at[1])
    slot = owner_one * 16 + rank_one % 16
    layer = rank_one // 16
    slot_one_ref[...] = jnp.concatenate([slot, layer], axis=0)
    slot_two_ref[...] = owner_two * 16 + rank_two
    feats = feats_ref[...].astype(f32).T
    wide = [jnp.where(layer == index, feats, 0.0) for index in range(4)]
    wide = jnp.concatenate(wide, axis=0).astype(bf16)
    send[...] = dot_nt(match(slot, 1024), wide).astype(bf16).reshape(PEERS, 16, 256)
    moved = exchange(me, send, rows_ref, sems.at[2], sems.at[3])
    marked.wait_recv()
    moved.wait_recv()
    marked.wait_send()
    moved.wait_send()


def front_kernel(
    rows_ref, places_ref, ident_ref, slot_ref, inlet_ref, outlet_ref, widen_ref, narrow_ref, pool_ref,
    send_ref, places_out, inputs_ref, mixed_ref, attended_ref, logs_ref, hidden_ref, slope_ref, pooled_ref, sizes_ref,
    total_ref,
):
    places, drops = spread_places(places_ref[...])
    for part in range(5):
        places_out[part : part + 1, :] = places[part]
    kept = [jnp.where(drop, -1, place) for place, drop in zip(places, drops)]
    hits = [match(place % 512, 512) for place in kept[:4]]
    last = last_senders([[place // 512 == patch for patch in range(PATCHES)] for place in kept[:4]], hits)
    kept_two = match(kept[4], COARSE)
    last_two = last_senders([[kept[4] >= 0]], [kept_two])
    places_out[5:6, :] = jnp.where(last_two[0], kept[4], -1)

    arrived = rows_ref[...].astype(f32).T
    landed = jnp.zeros((256, 512), f32)
    for layer in range(4):
        place = jnp.where(last[layer], kept[layer], -1)
        feats = arrived[64 * layer : 64 * layer + 64]
        wide = [jnp.where(place // 512 == patch, feats, 0.0) for patch in range(PATCHES)]
        wide = jnp.concatenate(wide, axis=0).astype(bf16)
        landed += dot_nt(wide, hits[layer])
    inputs_ref[...] = landed.astype(bf16).reshape(PATCHES, 64, PATCH)

    turned_weights = [turned(ref[...]) for ref in (inlet_ref, outlet_ref, widen_ref, narrow_ref)]
    total_ref[...] = jnp.zeros_like(total_ref)

    def step(patch, carry):
        result, mixed, attended, logs, hidden, slope = block_front(inputs_ref[patch], *turned_weights)
        mixed_ref[patch] = mixed
        attended_ref[patch] = attended
        logs_ref[patch] = jnp.concatenate(logs, axis=0)
        hidden_ref[patch] = hidden
        slope_ref[patch] = slope
        ident = ident_ref[:, pl.ds(pl.multiple_of(patch * PATCH, PATCH), PATCH)]
        counted = jnp.concatenate([result, jnp.ones((16, PATCH), bf16)], axis=0)
        total_ref[...] += dot_nt(counted, match(ident, COARSE))
        return carry

    lax.fori_loop(0, PATCHES, step, 0)
    sizes = total_ref[64:65]
    pooled = (total_ref[:64] / sizes).astype(bf16)
    pooled_ref[...] = pooled
    sizes_ref[...] = sizes
    coarse = dot(turned(pool_ref[...]), pooled).astype(bf16)
    send_ref[...] = dot_nt(match(slot_ref[...], 1024), coarse).astype(bf16)


def exchange_kernel(source_ref, target_ref, sems):
    me = lax.axis_index("pts")
    barrier = greet_peers(me)
    pl.semaphore_wait(barrier, PEERS - 1)
    moved = exchange(me, source_ref, target_ref, sems.at[0], sems.at[1])
    moved.wait_recv()
    moved.wait_send()


def store_lanes(ref, row, array):
    height = array.shape[0]
    for index in range(array.shape[1] // 128):
        start = row + height * index
        ref[start : start + height, :] = array[:, 128 * index : 128 * index + 128].astype(ref.dtype)


def middle_kernel(
    rows_ref, places_ref, cotangent_ref, inlet_ref, outlet_ref, widen_ref, narrow_ref,
    second_ref, send_ref, grads_ref,
):
    inputs = dot_nt(turned(rows_ref[...]), match(places_ref[5:6, :], COARSE)).astype(bf16)
    weights = [ref[...] for ref in (inlet_ref, outlet_ref, widen_ref, narrow_ref)]
    turned_weights = [turned(weight) for weight in weights]
    result, mixed, attended, logs, hidden, slope = block_front(inputs, *turned_weights)
    second_ref[...] = turned(result)
    gradient = turned(cotangent_ref[...])
    back, grad_inlet, grad_outlet, grad_widen, grad_narrow = block_back(
        inputs, mixed, attended, logs, hidden, slope, gradient, weights, turned_weights[1]
    )
    send_ref[...] = turned(dot(back, match(places_ref[4:5, :], COARSE)))
    store_lanes(grads_ref, 0, grad_inlet)
    store_lanes(grads_ref, 384, grad_outlet)
    store_lanes(grads_ref, 512, grad_widen)
    store_lanes(grads_ref, 1024, grad_narrow)


def back_kernel(
    rows_ref, slot_ref, places_ref, ident_ref, inputs_ref, mixed_ref, attended_ref, logs_ref, hidden_ref, slope_ref,
    pooled_ref, sizes_ref, inlet_ref, outlet_ref, widen_ref, narrow_ref, pool_ref,
    send_ref, grads_ref,
    back_ref, front_total, widen_total, narrow_total,
):
    grad_coarse = dot(turned(rows_ref[...]), match(slot_ref[...], 1024)).astype(bf16)
    grad_pool = dot_nt(pooled_ref[...], grad_coarse)
    grad_pooled = dot(pool_ref[...], grad_coarse).astype(bf16).astype(f32)
    share = (grad_pooled / sizes_ref[...]).astype(bf16)
    weights = [ref[...] for ref in (inlet_ref, outlet_ref, widen_ref, narrow_ref)]
    outlet_t = turned(weights[1])
    front_total[...] = jnp.zeros_like(front_total)
    widen_total[...] = jnp.zeros_like(widen_total)
    narrow_total[...] = jnp.zeros_like(narrow_total)

    def step(patch, carry):
        ident = ident_ref[:, pl.ds(pl.multiple_of(patch * PATCH, PATCH), PATCH)]
        gradient = dot(share, match(ident, COARSE)).astype(bf16)
        logs = [logs_ref[patch, head : head + 1, :] for head in range(4)]
        back, grad_inlet, grad_outlet, grad_widen, grad_narrow = block_back(
            inputs_ref[patch], mixed_ref[patch], attended_ref[patch], logs, hidden_ref[patch], slope_ref[patch],
            gradient, weights, outlet_t,
        )
        back_ref[patch] = back
        front_total[...] += jnp.concatenate([grad_inlet, grad_outlet], axis=1)
        widen_total[...] += grad_widen
        narrow_total[...] += grad_narrow
        return carry

    lax.fori_loop(0, PATCHES, step, 0)
    store_lanes(grads_ref, 0, front_total[...])
    store_lanes(grads_ref, 128, widen_total[...])
    store_lanes(grads_ref, 256, narrow_total[...])
    store_lanes(grads_ref, 384, grad_pool)
    grads_ref[448:, :] = jnp.zeros((64, 128), grads_ref.dtype)
    back = back_ref[...].reshape(256, PATCH)
    taken = []
    for layer in range(4):
        place = places_ref[layer : layer + 1, :]
        found = dot(back, match(place % 512, 512))
        parts = [jnp.where(place // 512 == patch, found[64 * patch : 64 * patch + 64], 0.0) for patch in range(PATCHES)]
        taken.append(parts[0] + parts[1] + parts[2] + parts[3])
    send_ref[...] = jnp.concatenate(taken, axis=0).T.astype(bf16)


def final_kernel(
    scale, source_ref, early_ref, late_ref, target_ref, out_ref,
    half, near, middle, far, chunk, whole, near_out, sems,
):
    me, rep = lax.axis_index("pts"), lax.axis_index("rep")
    place, core = me // 2, me % 2
    mine = core * 4 + rep

    def near_device(step):
        other = (mine + step) % NEAR
        return other, {"pts": place * 2 + other // 4, "rep": other % 4}

    def far_device(step):
        other = (place + step) % FAR
        return other, {"pts": other * 2 + core}

    def copy_to(source, target, index, device):
        return pltpu.make_async_remote_copy(
            source, target, sems.at[index], sems.at[index + 1], device_id=device, device_id_type=MESH
        )

    def batch_of(target, count, index):
        some = target.at[pl.ds(0, count - 1)]
        return copy_to(some, some, index, {"pts": me})

    barrier = greet_peers(me)

    def greet_near(step, carry):
        pl.semaphore_signal(barrier, device_id=near_device(step)[1], device_id_type=MESH)
        return carry

    lax.fori_loop(1, NEAR, greet_near, 0)
    half[:6] = early_ref[...]
    half[6:] = late_ref[...]
    pl.semaphore_wait(barrier, PEERS + NEAR - 2)

    def send_near(step, carry):
        other, device = near_device(step)
        copy_to(half.at[other], near.at[mine], 0, device).start()
        return carry

    lax.fori_loop(1, NEAR, send_near, 0)
    moved = exchange(me, source_ref, target_ref, sems.at[8], sems.at[9])
    near[mine] = half[mine]
    batch_near = batch_of(near, NEAR, 0)
    batch_near.wait_recv()
    total = near[0].astype(f32)
    for index in range(1, NEAR):
        total = total + near[index].astype(f32)
    middle[...] = total.reshape(FAR, 8, 128)

    def send_far(step, carry):
        other, device = far_device(step)
        copy_to(middle.at[other], far.at[place], 2, device).start()
        return carry

    lax.fori_loop(1, FAR, send_far, 0)
    far[place] = middle[place]
    batch_far = batch_of(far, FAR, 2)
    batch_far.wait_recv()
    chunk[...] = jnp.sum(far[...], axis=0) * scale

    def spread_far(step, carry):
        copy_to(chunk, whole.at[place], 4, far_device(step)[1]).start()
        return carry

    lax.fori_loop(1, FAR, spread_far, 0)
    whole[place] = chunk[...]
    batch_whole = batch_of(whole, FAR, 4)
    batch_whole.wait_recv()
    near_out[...] = whole[...].reshape(256, 128).astype(bf16)

    def spread_near(step, carry):
        copy_to(near_out, out_ref.at[mine], 6, near_device(step)[1]).start()
        return carry

    lax.fori_loop(1, NEAR, spread_near, 0)
    out_ref[mine] = near_out[...]
    batch_out = batch_of(out_ref, NEAR, 6)
    batch_out.wait_recv()
    moved.wait_recv()
    moved.wait_send()
    batch_near.wait_send()
    batch_far.wait_send()
    batch_whole.wait_send()
    batch_out.wait_send()


def load_lanes(ref, row, height, count):
    parts = [ref[row + height * index : row + height * (index + 1), :].astype(f32) for index in range(count)]
    return jnp.concatenate(parts, axis=1) if count > 1 else parts[0]


def output_kernel(
    rows_ref, slot_ref, grads_ref,
    feats_ref, inlet_one, outlet_one, widen_one, narrow_one, pool, inlet_two, outlet_two, widen_two, narrow_two,
):
    slot, layer = slot_ref[0:1, :], slot_ref[1:2, :]
    found = dot(turned(rows_ref[...]), match(slot, 1024))
    parts = [jnp.where(layer == index, found[64 * index : 64 * index + 64], 0.0) for index in range(4)]
    feats_ref[...] = (parts[0] + parts[1] + parts[2] + parts[3]).T.astype(bf16)
    front = load_lanes(grads_ref, 1536, 64, 2)
    inlet_one[...] = front[:, :192]
    outlet_one[...] = front[:, 192:]
    widen_one[...] = load_lanes(grads_ref, 1664, 64, 2)
    narrow_one[...] = load_lanes(grads_ref, 1792, 64, 2).T
    pool[...] = load_lanes(grads_ref, 1920, 64, 1)
    inlet_two[...] = load_lanes(grads_ref, 0, 128, 3)
    outlet_two[...] = load_lanes(grads_ref, 384, 128, 1)
    widen_two[...] = load_lanes(grads_ref, 512, 128, 4)
    narrow_two[...] = load_lanes(grads_ref, 1024, 128, 4).T


def call(kernel, outs, scratch, *operands, collective=None):
    params = {} if collective is None else {"collective_id": collective, "has_side_effects": True}
    whole = pl.BlockSpec(memory_space=pltpu.VMEM)
    return pl.pallas_call(
        kernel,
        out_shape=[jax.ShapeDtypeStruct(shape, dtype) for shape, dtype in outs],
        in_specs=[whole] * len(operands),
        out_specs=[whole] * len(outs),
        scratch_shapes=scratch,
        compiler_params=pltpu.CompilerParams(vmem_limit_bytes=56 * 2**20, **params),
    )(*operands)


def shards(
    feats,
    dest_first,
    pool_ids,
    dest_second,
    cotangent,
    inlet_first,
    outlet_first,
    widen_first,
    narrow_first,
    pool_weight,
    inlet_second,
    outlet_second,
    widen_second,
    narrow_second,
):
    first = (inlet_first, outlet_first, widen_first, narrow_first)
    second = (inlet_second, outlet_second, widen_second, narrow_second)
    rows, places, slot_one, slot_two = call(
        pack_kernel,
        [((PEERS, 16, 256), bf16), ((PEERS, 1, 128), f32), ((2, ROWS), i32), ((1, COARSE), i32)],
        [
            pltpu.VMEM((PEERS, 16, 256), bf16),
            pltpu.VMEM((PEERS, 1, 128), f32),
            pltpu.SemaphoreType.DMA((4,)),
        ],
        feats[0], dest_first, dest_second,
        collective=1,
    )
    send, places, *saved = call(
        front_kernel,
        [
            ((1024, 128), bf16),
            ((6, 1024), i32),
            ((PATCHES, 64, PATCH), bf16),
            ((PATCHES, 192, PATCH), bf16),
            ((PATCHES, 64, PATCH), bf16),
            ((PATCHES, 4, PATCH), f32),
            ((PATCHES, 256, PATCH), bf16),
            ((PATCHES, 256, PATCH), bf16),
            ((64, COARSE), bf16),
            ((1, COARSE), f32),
        ],
        [pltpu.VMEM((80, COARSE), f32)],
        rows.reshape(1024, 256), places.reshape(PEERS, 128), pool_ids, slot_two, *first, pool_weight,
    )

    def move(array, collective):
        return call(
            exchange_kernel,
            [((PEERS, 16, 128), bf16)],
            [pltpu.SemaphoreType.DMA((2,))],
            array.reshape(PEERS, 16, 128),
            collective=collective,
        )[0].reshape(1024, 128)

    second_out, send, grads_second = call(
        middle_kernel,
        [((COARSE, 128), bf16), ((1024, 128), bf16), ((1536, 128), bf16)],
        [],
        move(send, 2), places, cotangent[0], *second,
    )
    send, grads_first = call(
        back_kernel,
        [((1024, 256), bf16), ((512, 128), bf16)],
        [
            pltpu.VMEM((PATCHES, 64, PATCH), bf16),
            pltpu.VMEM((64, 256), f32),
            pltpu.VMEM((64, 256), f32),
            pltpu.VMEM((64, 256), f32),
        ],
        move(send, 3), slot_two, places, pool_ids, *saved, *first, pool_weight,
    )
    scale = 1.0 / math.sqrt(lax.axis_size("rep") * lax.axis_size("pts") * COARSE)
    rows, grads = call(
        lambda *refs: final_kernel(scale, *refs),
        [((PEERS, 16, 256), bf16), ((NEAR, 256, 128), bf16)],
        [
            pltpu.VMEM((NEAR, 256, 128), bf16),
            pltpu.VMEM((NEAR, 256, 128), bf16),
            pltpu.VMEM((FAR, 8, 128), f32),
            pltpu.VMEM((FAR, 8, 128), f32),
            pltpu.VMEM((8, 128), f32),
            pltpu.VMEM((FAR, 8, 128), f32),
            pltpu.VMEM((256, 128), bf16),
            pltpu.SemaphoreType.DMA((10,)),
        ],
        send.reshape(PEERS, 16, 256), grads_second.reshape(6, 256, 128), grads_first.reshape(2, 256, 128),
        collective=4,
    )
    feats_grad, *totals = call(
        output_kernel,
        [((ROWS, 64), bf16)]
        + [
            (weight.shape, f32)
            for weight in first + (pool_weight,) + second
        ],
        [],
        rows.reshape(1024, 256), slot_one, grads.reshape(2048, 128),
    )
    return (second_out[None], feats_grad[None], *totals)


def solution(mesh):
    split = P("rep", "pts")
    return jax.shard_map(
        shards,
        mesh=mesh,
        in_specs=(split,) * 5 + (P(),) * 9,
        out_specs=(split,) * 2 + (P(),) * 9,
        check_vma=False,
    )
```

```python
import math

import jax
import jax.numpy as jnp
from jax import lax
from jax.experimental import pallas as pl
from jax.experimental.pallas import tpu as pltpu
from jax.sharding import PartitionSpec as P


HEAD = 16
PATCH = 512
PATCHES = 4
ROWS = 2048
COARSE = 512
PEERS = 64
NEAR, FAR = 8, 32
MESH = pl.DeviceIdType.MESH
SHARPEN = HEAD**-0.5 / math.log(2.0)
f32, bf16, i32 = jnp.float32, jnp.bfloat16, jnp.int32


def dot(left, right):
    return jnp.dot(left, right, preferred_element_type=f32)


def dot_nt(left, right):
    return lax.dot_general(left, right, (((1,), (1,)), ((), ())), preferred_element_type=f32)


def turned(array):
    return array.astype(f32).T.astype(bf16)


def rows_of(count, width):
    return lax.broadcasted_iota(i32, (count, width), 0)


def match(row, count):
    return jnp.where(rows_of(count, row.shape[1]) == row, 1.0, 0.0).astype(bf16)


def norm(values):
    centred = values - jnp.mean(values, axis=0, keepdims=True)
    rate = lax.rsqrt(jnp.mean(centred * centred, axis=0, keepdims=True) + 1e-05)
    return centred * rate, rate


def norm_back(gradient, normed, rate):
    mean = jnp.mean(gradient, axis=0, keepdims=True)
    along = jnp.mean(gradient * normed, axis=0, keepdims=True)
    return rate * (gradient - mean - normed * along)


def padded(rows, head, width):
    parts = [rows]
    if head > 0:
        parts.insert(0, jnp.zeros((HEAD * head, rows.shape[1]), rows.dtype))
    rest = width - HEAD * (head + 1)
    if rest > 0:
        parts.append(jnp.zeros((rest, rows.shape[1]), rows.dtype))
    return jnp.concatenate(parts, axis=0)


def only(array, head):
    return padded(array[HEAD * head : HEAD * (head + 1)], head, array.shape[0])


def attend(mixed, width, powers_ref, first_power):
    keys = turned(mixed[width : 2 * width])
    ones = jnp.ones((HEAD, PATCH), bf16)
    outs, shares = [], []
    for head in range(width // HEAD):
        scores = dot(keys, only(mixed[:width], head))
        top = jnp.max(scores, axis=0, keepdims=True)
        powers = jnp.exp2((scores - top) * SHARPEN).astype(bf16)
        powers_ref[first_power + head] = powers
        start = 2 * width + HEAD * head
        sums = dot(jnp.concatenate([mixed[start : start + HEAD], ones], axis=0), powers)
        share = 1.0 / sums[HEAD : HEAD + 1]
        outs.append(sums[:HEAD] * share)
        shares.append(share)
    return jnp.concatenate(outs, axis=0).astype(bf16), jnp.concatenate(shares, axis=0)


def attend_back(mixed, attended, gradient, shares, width, powers_ref, first_power):
    keys = turned(mixed[width : 2 * width])
    values = turned(mixed[2 * width :])
    grad_queries, grad_keys, grad_values = [], [], []
    for head in range(width // HEAD):
        part = slice(HEAD * head, HEAD * (head + 1))
        queries = mixed[part]
        key_rows = mixed[width + HEAD * head : width + HEAD * (head + 1)]
        shared = gradient[part] * shares[head : head + 1]
        overlap = jnp.sum(shared * attended[part].astype(f32), axis=0, keepdims=True)
        shared = shared.astype(bf16)
        powers = powers_ref[first_power + head]
        spread = dot(values, padded(shared, head, width))
        change = (powers.astype(f32) * (spread - overlap)).astype(bf16)
        grad_queries.append(dot(key_rows, change) * HEAD**-0.5)
        grad_keys.append(dot_nt(queries, change) * HEAD**-0.5)
        grad_values.append(dot_nt(shared, powers))
    return jnp.concatenate(grad_queries + grad_keys + grad_values, axis=0).astype(bf16)


def block_front(inputs, inlet_t, outlet_t, widen_t, narrow_t, powers_ref, first_power):
    width = inputs.shape[0]
    start = inputs.astype(f32)
    normed = norm(start)[0].astype(bf16)
    mixed = dot(inlet_t, normed).astype(bf16)
    attended, shares = attend(mixed, width, powers_ref, first_power)
    middle = start + dot(outlet_t, attended)
    second = norm(middle)[0].astype(bf16)
    values = dot(widen_t, second)
    below = 0.5 + 0.5 * lax.erf(values * math.sqrt(0.5))
    hidden = (values * below).astype(bf16)
    result = (middle + dot(narrow_t, hidden)).astype(bf16)
    return result, mixed, attended, shares, hidden, values, below


def gelu_slope(values, below):
    bell = jnp.exp(-0.5 * values * values) * (1.0 / math.sqrt(2.0 * math.pi))
    return (below + values * bell).astype(bf16)


def block_back(inputs, mixed, attended, shares, hidden, slope, gradient, weights, outlet_t, powers_ref, first_power):
    inlet, outlet, widen, narrow = weights
    width = inputs.shape[0]
    start = inputs.astype(f32)
    normed, rate = norm(start)
    second, rate_two = norm(start + dot(outlet_t, attended))
    grad_wide = (dot(narrow, gradient) * slope.astype(f32)).astype(bf16)
    grad_middle = gradient.astype(f32) + norm_back(dot(widen, grad_wide), second, rate_two)
    short = grad_middle.astype(bf16)
    grad_mixed = attend_back(mixed, attended, dot(outlet, short), shares, width, powers_ref, first_power)
    grad_inputs = grad_middle + norm_back(dot(inlet, grad_mixed), normed, rate)

    def weight_grads():
        return (
            dot_nt(normed.astype(bf16), grad_mixed),
            dot_nt(attended, short),
            dot_nt(second.astype(bf16), grad_wide),
            dot_nt(gradient, hidden),
        )

    return grad_inputs.astype(bf16), weight_grads


def ranks(owner):
    before_me = jnp.where(rows_of(256, 256) < lax.broadcasted_iota(i32, (256, 256), 1), 1.0, 0.0)
    before_me = before_me.astype(bf16)
    before = jnp.zeros((PEERS, 1), f32)
    found = []
    for start in range(0, owner.shape[1], 256):
        hits = jnp.where(rows_of(PEERS, 256) == owner[:, start : start + 256], 1.0, 0.0)
        count = dot(hits.astype(bf16), before_me) + before
        found.append(jnp.sum(hits * count, axis=0, keepdims=True))
        before = before + jnp.sum(hits, axis=1, keepdims=True)
    return jnp.concatenate(found, axis=1).astype(i32)


def marks(owner, rank, value):
    hits = match(owner, PEERS)
    at = rows_of(128, owner.shape[1]) == rank
    high = jnp.where(at, (value >> 6).astype(f32), 0.0).astype(bf16)
    low = jnp.where(at, (value & 63).astype(f32), 0.0).astype(bf16)
    return dot_nt(hits, high) * 64.0 + dot_nt(hits, low)


def spread_places(table):
    lane = lax.broadcasted_iota(i32, (PEERS, 128), 1)
    apart = table + jnp.where(lane >= 64, 4096.0, 0.0)
    over = jnp.zeros((PEERS, 128), f32)
    for shift in range(1, 64):
        over = jnp.where(apart == pltpu.roll(apart, 128 - shift, 1), 1.0, over)
    high = jnp.floor(table * (1.0 / 64.0))
    low = table - 64.0 * high
    high = high + 64.0 * over
    stack = []
    for part in range(5):
        stack += [high[:, 16 * part : 16 * part + 16], low[:, 16 * part : 16 * part + 16]]
    stack = jnp.concatenate(stack, axis=0).astype(bf16)
    column = lax.broadcasted_iota(i32, (16, 1024), 1)
    spread = dot(stack, jnp.where(column % 16 == rows_of(16, 1024), 1.0, 0.0).astype(bf16))
    own = rows_of(PEERS, 1024) == lax.broadcasted_iota(i32, (PEERS, 1024), 1) // 16
    places, drops = [], []
    for part in range(5):
        high = jnp.sum(jnp.where(own, spread[128 * part : 128 * part + 64], 0.0), axis=0, keepdims=True)
        low = jnp.sum(jnp.where(own, spread[128 * part + 64 : 128 * part + 128], 0.0), axis=0, keepdims=True)
        drops.append(high > 63.5)
        high = jnp.where(high > 63.5, high - 64.0, high)
        places.append((high * 64.0 + low).astype(i32) - 1)
    return places, drops


def last_senders(inside, hits):
    width = hits[0].shape[0]
    count = len(inside[0])
    sender = lax.broadcasted_iota(i32, (1, 1024), 1) // 16
    own = rows_of(PEERS, 1024) == sender
    seen = jnp.zeros((PEERS * count, width), f32)
    for masks, hit in zip(inside, hits):
        wide = [jnp.where(own & mask, 1.0, 0.0) for mask in masks]
        seen += dot_nt(jnp.concatenate(wide, axis=0).astype(bf16), hit)
    index = rows_of(PEERS, width).astype(f32)
    lasts = []
    for part in range(count):
        lasts.append(jnp.max(jnp.where(seen[PEERS * part : PEERS * part + PEERS] > 0.5, index, -1.0), axis=0, keepdims=True))
    lasts = jnp.concatenate(lasts + [jnp.zeros((16 - count, width), f32)], axis=0).astype(bf16)
    found = []
    for masks, hit in zip(inside, hits):
        got = dot(lasts, hit)
        mine = jnp.full((1, 1024), -1.0, f32)
        for part in range(count):
            mine = jnp.where(masks[part], got[part : part + 1], mine)
        found.append(mine == sender.astype(f32))
    return found


def greet_peers(me):
    barrier = pltpu.get_barrier_semaphore()

    def greet(step, carry):
        pl.semaphore_signal(
            barrier, device_id={"pts": (me + step) % PEERS}, device_id_type=MESH
        )
        return carry

    lax.fori_loop(1, PEERS, greet, 0)
    return barrier


def send_to(source, target, sems, index, device):
    return pltpu.make_async_remote_copy(
        source, target, sems.at[index], sems.at[index + 1], device_id=device, device_id_type=MESH
    )


def batch_of(me, target, count, sems, index):
    some = target.at[pl.ds(0, count - 1)]
    return send_to(some, some, sems, index, {"pts": me})


def exchange(me, source, target, sems, index):

    def send(step, carry):
        other = (me + step) % PEERS
        send_to(source.at[other], target.at[me], sems, index, {"pts": other}).start()
        return carry

    lax.fori_loop(1, PEERS, send, 0)
    target[me] = source[me]
    return batch_of(me, target, PEERS, sems, index)


def exchange_parts(me, make_part, source, target, sems, index):
    for turn in range(4):
        quarter = (me // 16 + turn) % 4
        source[pl.ds(16 * quarter, 16)] = make_part(quarter)

        def send(step, carry, quarter=quarter):
            other = 16 * quarter + (me + step) % 16
            send_to(source.at[other], target.at[me], sems, index, {"pts": other}).start()
            return carry

        lax.fori_loop(1 if turn == 0 else 0, 16, send, 0)
    target[me] = source[me]
    return batch_of(me, target, PEERS, sems, index)


class Adder:
    def __init__(self, scale, half, near, middle, far, chunk, whole, flat, near_out, out, sems, index):
        self.scale, self.half, self.near, self.middle, self.far = scale, half, near, middle, far
        self.chunk, self.whole, self.flat, self.near_out, self.out = chunk, whole, flat, near_out, out
        self.sems, self.index, self.unit = sems, index, chunk.shape[0]
        self.me, rep = lax.axis_index("pts"), lax.axis_index("rep")
        self.place, self.core = self.me // 2, self.me % 2
        self.mine = self.core * 4 + rep

    def near_device(self, step):
        other = (self.mine + step) % NEAR
        return other, {"pts": self.place * 2 + other // 4, "rep": other % 4}

    def far_device(self, step):
        other = (self.place + step) % FAR
        return other, {"pts": other * 2 + self.core}

    def batch(self, target, count, stage):
        return batch_of(self.me, target, count, self.sems, self.index + 2 * stage)

    def loop(self, count, source, target, stage, device_of):
        def send(step, carry):
            other, device = device_of(step)
            block = source.at[other] if source.shape[0] == count and len(source.shape) == 3 else source
            send_to(block, target, self.sems, self.index + 2 * stage, device).start()
            return carry

        lax.fori_loop(1, count, send, 0)

    def send_near(self):
        self.loop(NEAR, self.half, self.near.at[self.mine], 0, self.near_device)
        self.near[self.mine] = self.half[self.mine]

    def send_far(self):
        self.batch(self.near, NEAR, 0).wait_recv()
        total = self.near[0].astype(f32)
        for index in range(1, NEAR):
            total = total + self.near[index].astype(f32)
        for index in range(FAR):
            self.middle[index] = total[self.unit * index : self.unit * (index + 1)]
        self.loop(FAR, self.middle, self.far.at[self.place], 1, self.far_device)
        self.far[self.place] = self.middle[self.place]

    def spread_far(self):
        self.batch(self.far, FAR, 1).wait_recv()
        self.chunk[...] = jnp.sum(self.far[...], axis=0) * self.scale
        self.loop(FAR, self.chunk, self.whole.at[self.place], 2, self.far_device)
        self.whole[self.place] = self.chunk[...]

    def spread_near(self):
        self.batch(self.whole, FAR, 2).wait_recv()
        for index in range(FAR):
            self.flat[self.unit * index : self.unit * (index + 1), :] = self.whole[index]
        self.near_out[...] = self.flat[...].astype(bf16)
        self.loop(NEAR, self.near_out, self.out.at[self.mine], 3, self.near_device)
        self.out[self.mine] = self.near_out[...]

    def end(self):
        self.batch(self.out, NEAR, 3).wait_recv()
        self.batch(self.near, NEAR, 0).wait_send()
        self.batch(self.far, FAR, 1).wait_send()
        self.batch(self.whole, FAR, 2).wait_send()
        self.batch(self.out, NEAR, 3).wait_send()


def adder_scratch(rows):
    unit = rows // FAR
    return [
        pltpu.VMEM((NEAR, rows, 128), bf16),
        pltpu.VMEM((NEAR, rows, 128), bf16),
        pltpu.VMEM((FAR, unit, 128), f32),
        pltpu.VMEM((FAR, unit, 128), f32),
        pltpu.VMEM((unit, 128), f32),
        pltpu.VMEM((FAR, unit, 128), f32),
        pltpu.VMEM((rows, 128), f32),
        pltpu.VMEM((rows, 128), bf16),
    ]


def store_lanes(ref, row, array):
    height, block = array.shape[0], ref.shape[1]
    for index in range(array.shape[1] // 128):
        part = array[:, 128 * index : 128 * index + 128].astype(ref.dtype)
        start, done = row + height * index, 0
        while done < height:
            count = min(height - done, block - (start + done) % block)
            inside = (start + done) % block
            ref[(start + done) // block, inside : inside + count, :] = part[done : done + count]
            done += count


def load_lanes(ref, row, height, count):
    parts = [ref[row + height * index : row + height * (index + 1), :].astype(f32) for index in range(count)]
    return jnp.concatenate(parts, axis=1) if count > 1 else parts[0]


def main_kernel(
    scale,
    feats_ref, first_ref, ident_ref, second_ref, cotangent_ref,
    inlet_one, outlet_one, widen_one, narrow_one_t, pool_ref, inlet_two, outlet_two, widen_two, narrow_two,
    second_out, feats_out, sums_one, sums_two,
    mark, marks_in, send_one, rows_one, send_two, rows_two, send_three, rows_three, send_four, rows_four,
    places_ref, inputs_ref, mixed_ref, attended_ref, shares_ref, hidden_ref, values_ref, below_ref, slope_ref,
    powers_one, powers_two, total_ref, back_ref, front_total, widen_total, narrow_total, *rest,
):
    me = lax.axis_index("pts")
    sems = rest[-1]
    late = Adder(scale, *rest[:8], sums_one, sems, 10)
    early = Adder(scale, *rest[8:16], sums_two, sems, 18)
    barrier = greet_peers(me)

    def greet_near(step, carry):
        pl.semaphore_signal(barrier, device_id=early.near_device(step)[1], device_id_type=MESH)
        return carry

    lax.fori_loop(1, NEAR, greet_near, 0)

    first, second = first_ref[...], second_ref[...]
    owner_one, owner_two = first // ROWS, second // COARSE
    rank_one, rank_two = ranks(owner_one), ranks(owner_two)
    found = marks(owner_one, rank_one, first % ROWS + 1)
    found += marks(owner_two, rank_two + 64, second % COARSE + 1)
    mark[:, 0, :] = found
    slot_one, layer_one = owner_one * 16 + rank_one % 16, rank_one // 16
    slot_two = owner_two * 16 + rank_two
    feats = feats_ref[...].astype(f32)
    wide = [jnp.where(layer_one == index, feats, 0.0) for index in range(4)]
    wide = jnp.concatenate(wide, axis=0).astype(bf16)
    pl.semaphore_wait(barrier, PEERS + NEAR - 2)
    marked = exchange(me, mark, marks_in, sems, 0)

    def pack(quarter):
        return dot_nt(match(slot_one - 256 * quarter, 256), wide).astype(bf16).reshape(16, 16, 256)

    moved_one = exchange_parts(me, pack, send_one, rows_one, sems, 2)

    marked.wait_recv()
    places, drops = spread_places(marks_in[:, 0, :])
    for part in range(5):
        places_ref[part : part + 1, :] = places[part]
    kept = [jnp.where(drop, -1, place) for place, drop in zip(places, drops)]
    hits = [match(place % 512, 512) for place in kept[:4]]
    last = last_senders([[place // 512 == patch for patch in range(PATCHES)] for place in kept[:4]], hits)
    last_two = last_senders([[kept[4] >= 0]], [match(kept[4], COARSE)])
    places_ref[5:6, :] = jnp.where(last_two[0], kept[4], -1)
    weights_one = [inlet_one[...], outlet_one[...], widen_one[...], turned(narrow_one_t[...])]
    turned_one = [turned(weight) for weight in weights_one[:3]] + [narrow_one_t[...]]

    moved_one.wait_recv()
    arrived = rows_one[...].reshape(1024, 256).astype(f32).T
    landed = jnp.zeros((256, 512), f32)
    for layer in range(4):
        place = jnp.where(last[layer], kept[layer], -1)
        points = arrived[64 * layer : 64 * layer + 64]
        spread = [jnp.where(place // 512 == patch, points, 0.0) for patch in range(PATCHES)]
        landed += dot_nt(jnp.concatenate(spread, axis=0).astype(bf16), hits[layer])
    inputs_ref[...] = landed.astype(bf16).reshape(PATCHES, 64, PATCH)
    total_ref[...] = jnp.zeros_like(total_ref)

    def ident_of(patch):
        return ident_ref[:, pl.ds(pl.multiple_of(patch * PATCH, PATCH), PATCH)]

    def front(patch, carry):
        result, mixed, attended, shares, hidden, values, below = block_front(
            inputs_ref[patch], *turned_one, powers_one, 4 * patch
        )
        mixed_ref[patch] = mixed
        attended_ref[patch] = attended
        shares_ref[patch] = shares
        hidden_ref[patch] = hidden
        values_ref[patch] = values
        below_ref[patch] = below
        counted = jnp.concatenate([result, jnp.ones((16, PATCH), bf16)], axis=0)
        total_ref[...] += dot_nt(counted, match(ident_of(patch), COARSE))
        return carry

    lax.fori_loop(0, PATCHES, front, 0)
    sizes = total_ref[64:65]
    pooled = (total_ref[:64] / sizes).astype(bf16)
    coarse = dot(turned(pool_ref[...]), pooled).astype(bf16)
    send_two[...] = dot_nt(match(slot_two, 1024), coarse).astype(bf16).reshape(PEERS, 16, 128)
    moved_two = exchange(me, send_two, rows_two, sems, 4)

    def slopes(patch, carry):
        slope_ref[patch] = gelu_slope(values_ref[patch], below_ref[patch])
        return carry

    lax.fori_loop(0, PATCHES, slopes, 0)
    weights_two = [inlet_two[...], outlet_two[...], widen_two[...], narrow_two[...]]
    turned_two = [turned(weight) for weight in weights_two]
    gradient = turned(cotangent_ref[...])
    landing = match(places_ref[5:6, :], COARSE)
    moved_two.wait_recv()

    inputs = dot_nt(turned(rows_two[...].reshape(1024, 128)), landing).astype(bf16)
    result, mixed, attended, shares, hidden, values, below = block_front(inputs, *turned_two, powers_two, 0)
    back, grads_of = block_back(
        inputs, mixed, attended, shares, hidden, gelu_slope(values, below), gradient,
        weights_two, turned_two[1], powers_two, 0,
    )
    send_three[...] = turned(dot(back, match(places_ref[4:5, :], COARSE))).reshape(PEERS, 16, 128)
    moved_three = exchange(me, send_three, rows_three, sems, 6)
    row = 0
    for grad in grads_of():
        store_lanes(early.half, row, grad)
        row += grad.shape[0] * grad.shape[1] // 128
    early.half[6:] = jnp.zeros((2, 256, 128), bf16)
    early.send_near()
    second_out[...] = turned(result)
    front_total[...] = jnp.zeros_like(front_total)
    widen_total[...] = jnp.zeros_like(widen_total)
    narrow_total[...] = jnp.zeros_like(narrow_total)
    taking = match(slot_two, 1024)
    moved_three.wait_recv()

    grad_coarse = dot(turned(rows_three[...].reshape(1024, 128)), taking).astype(bf16)
    grad_pool = dot_nt(pooled, grad_coarse)
    grad_pooled = dot(pool_ref[...], grad_coarse).astype(bf16).astype(f32)
    share = (grad_pooled / sizes).astype(bf16)

    def rear(patch, carry):
        gradient = dot(share, match(ident_of(patch), COARSE)).astype(bf16)
        back, grads_of = block_back(
            inputs_ref[patch], mixed_ref[patch], attended_ref[patch], shares_ref[patch], hidden_ref[patch],
            slope_ref[patch], gradient, weights_one, turned_one[1], powers_one, 4 * patch,
        )
        back_ref[patch] = back
        grad_inlet, grad_outlet, grad_widen, grad_narrow = grads_of()
        front_total[...] += jnp.concatenate([grad_inlet, grad_outlet], axis=1)
        widen_total[...] += grad_widen
        narrow_total[...] += grad_narrow
        pl.when(patch == 0)(early.send_far)
        pl.when(patch == 1)(early.spread_far)
        pl.when(patch == 2)(early.spread_near)
        return carry

    lax.fori_loop(0, PATCHES, rear, 0)
    store_lanes(late.half, 0, front_total[...])
    store_lanes(late.half, 128, widen_total[...])
    store_lanes(late.half, 256, narrow_total[...])
    store_lanes(late.half, 384, grad_pool)
    late.half[7] = jnp.zeros((64, 128), bf16)
    late.send_near()
    back = back_ref[...].reshape(256, PATCH)

    def take(quarter):
        taken = []
        for layer in range(4):
            place = places_ref[layer : layer + 1, pl.ds(pl.multiple_of(quarter * 256, 256), 256)]
            found = dot(back, match(place % 512, 512))
            parts = [
                jnp.where(place // 512 == patch, found[64 * patch : 64 * patch + 64], 0.0) for patch in range(PATCHES)
            ]
            taken.append(parts[0] + parts[1] + parts[2] + parts[3])
        return jnp.concatenate(taken, axis=0).T.astype(bf16).reshape(16, 16, 256)

    moved_four = exchange_parts(me, take, send_four, rows_four, sems, 8)
    late.send_far()
    picking = match(slot_one, 1024)
    late.spread_far()
    late.spread_near()
    moved_four.wait_recv()
    found = dot(turned(rows_four[...].reshape(1024, 256)), picking)
    parts = [jnp.where(layer_one == index, found[64 * index : 64 * index + 64], 0.0) for index in range(4)]
    feats_out[...] = (parts[0] + parts[1] + parts[2] + parts[3]).astype(bf16)
    early.end()
    late.end()
    marked.wait_send()
    moved_one.wait_send()
    moved_two.wait_send()
    moved_three.wait_send()
    moved_four.wait_send()


def output_kernel(
    second_in, feats_in, late_ref, early_ref,
    second_out, feats_out, inlet_one, outlet_one, widen_one, narrow_one_t, pool,
    inlet_two, outlet_two, widen_two, narrow_two,
):
    second_out[...] = second_in[...]
    feats_out[...] = feats_in[...]
    front = load_lanes(late_ref, 0, 64, 2)
    inlet_one[...] = front[:, :192]
    outlet_one[...] = front[:, 192:]
    widen_one[...] = load_lanes(late_ref, 128, 64, 2)
    narrow_one_t[...] = load_lanes(late_ref, 256, 64, 2)
    pool[...] = load_lanes(late_ref, 384, 64, 1)
    inlet_two[...] = load_lanes(early_ref, 0, 128, 3)
    outlet_two[...] = load_lanes(early_ref, 384, 128, 1)
    widen_two[...] = load_lanes(early_ref, 512, 128, 4)
    narrow_two[...] = load_lanes(early_ref, 1024, 128, 4).T


def call(kernel, outs, scratch, *operands, collective=None):
    params = {} if collective is None else {"collective_id": collective, "has_side_effects": True}
    whole = pl.BlockSpec(memory_space=pltpu.VMEM)
    return pl.pallas_call(
        kernel,
        out_shape=[jax.ShapeDtypeStruct(shape, dtype) for shape, dtype in outs],
        in_specs=[whole] * len(operands),
        out_specs=[whole] * len(outs),
        scratch_shapes=scratch,
        compiler_params=pltpu.CompilerParams(vmem_limit_bytes=56 * 2**20, **params),
    )(*operands)


def shards(
    feats,
    dest_first,
    pool_ids,
    dest_second,
    cotangent,
    inlet_first,
    outlet_first,
    widen_first,
    narrow_first,
    pool_weight,
    inlet_second,
    outlet_second,
    widen_second,
    narrow_second,
):
    scale = 1.0 / math.sqrt(lax.axis_size("rep") * lax.axis_size("pts") * COARSE)
    wide_slots, slots = pltpu.VMEM((PEERS, 16, 256), bf16), pltpu.VMEM((PEERS, 16, 128), bf16)
    mark = pltpu.VMEM((PEERS, 1, 128), f32)
    moved = call(
        lambda *refs: main_kernel(scale, *refs),
        [((COARSE, 128), bf16), ((64, ROWS), bf16), ((NEAR, 64, 128), bf16), ((NEAR, 256, 128), bf16)],
        [mark, mark, wide_slots, wide_slots, slots, slots, slots, slots, wide_slots, wide_slots]
        + [
            pltpu.VMEM((6, 1024), i32),
            pltpu.VMEM((PATCHES, 64, PATCH), bf16),
            pltpu.VMEM((PATCHES, 192, PATCH), bf16),
            pltpu.VMEM((PATCHES, 64, PATCH), bf16),
            pltpu.VMEM((PATCHES, 4, PATCH), f32),
            pltpu.VMEM((PATCHES, 256, PATCH), bf16),
            pltpu.VMEM((PATCHES, 256, PATCH), f32),
            pltpu.VMEM((PATCHES, 256, PATCH), f32),
            pltpu.VMEM((PATCHES, 256, PATCH), bf16),
            pltpu.VMEM((16, PATCH, PATCH), bf16),
            pltpu.VMEM((8, PATCH, PATCH), bf16),
            pltpu.VMEM((80, COARSE), f32),
            pltpu.VMEM((PATCHES, 64, PATCH), bf16),
            pltpu.VMEM((64, 256), f32),
            pltpu.VMEM((64, 256), f32),
            pltpu.VMEM((64, 256), f32),
        ]
        + adder_scratch(64)
        + adder_scratch(256)
        + [pltpu.SemaphoreType.DMA((26,))],
        feats[0].T, dest_first, pool_ids, dest_second, cotangent[0],
        inlet_first, outlet_first, widen_first, narrow_first.T, pool_weight,
        inlet_second, outlet_second, widen_second, narrow_second,
        collective=1,
    )
    second_out, feats_grad, late, early = moved
    weights = (inlet_first, outlet_first, widen_first, narrow_first.T, pool_weight)
    weights += (inlet_second, outlet_second, widen_second, narrow_second)
    second_out, feats_grad, *totals = call(
        output_kernel,
        [((COARSE, 128), bf16), ((64, ROWS), bf16)] + [(weight.shape, f32) for weight in weights],
        [],
        second_out, feats_grad, late.reshape(512, 128), early.reshape(2048, 128),
    )
    totals[3] = totals[3].T
    return (second_out[None], feats_grad.T[None], *totals)


def solution(mesh):
    split = P("rep", "pts")
    return jax.shard_map(
        shards,
        mesh=mesh,
        in_specs=(split,) * 5 + (P(),) * 9,
        out_specs=(split,) * 2 + (P(),) * 9,
        check_vma=False,
    )
```

```python
import math

import jax
import jax.numpy as jnp
from jax import lax
from jax.experimental import pallas as pl
from jax.experimental.pallas import tpu as pltpu
from jax.sharding import PartitionSpec as P


HEAD = 16
PATCH = 512
PATCHES = 4
ROWS = 2048
COARSE = 512
PEERS = 64
NEAR, FAR = 32, 8
MESH = pl.DeviceIdType.MESH
SHARPEN = HEAD**-0.5 / math.log(2.0)
f32, bf16, i32 = jnp.float32, jnp.bfloat16, jnp.int32


def dot(left, right):
    return jnp.dot(left, right, preferred_element_type=f32)


def dot_nt(left, right):
    return lax.dot_general(left, right, (((1,), (1,)), ((), ())), preferred_element_type=f32)


def turned(array):
    return array.astype(f32).T.astype(bf16)


def rows_of(count, width):
    return lax.broadcasted_iota(i32, (count, width), 0)


def match(row, count):
    return jnp.where(rows_of(count, row.shape[1]) == row, 1.0, 0.0).astype(bf16)


def norm(values):
    centred = values - jnp.mean(values, axis=0, keepdims=True)
    rate = lax.rsqrt(jnp.mean(centred * centred, axis=0, keepdims=True) + 1e-05)
    return centred * rate, rate


def norm_back(gradient, normed, rate):
    mean = jnp.mean(gradient, axis=0, keepdims=True)
    along = jnp.mean(gradient * normed, axis=0, keepdims=True)
    return rate * (gradient - mean - normed * along)


def padded(rows, head, width):
    parts = [rows]
    if head > 0:
        parts.insert(0, jnp.zeros((HEAD * head, rows.shape[1]), rows.dtype))
    rest = width - HEAD * (head + 1)
    if rest > 0:
        parts.append(jnp.zeros((rest, rows.shape[1]), rows.dtype))
    return jnp.concatenate(parts, axis=0)


def only(array, head):
    return padded(array[HEAD * head : HEAD * (head + 1)], head, array.shape[0])


def attend(mixed, width, powers_ref, first_power):
    keys = turned(mixed[width : 2 * width])
    ones = jnp.ones((HEAD, PATCH), bf16)
    outs, shares = [], []
    later = dot(keys, only(mixed[:width], 0))
    for head in range(width // HEAD):
        scores = later
        if head + 1 < width // HEAD:
            later = dot(keys, only(mixed[:width], head + 1))
        top = jnp.max(scores, axis=0, keepdims=True)
        powers = jnp.exp2((scores - top) * SHARPEN).astype(bf16)
        powers_ref[first_power + head] = powers
        start = 2 * width + HEAD * head
        sums = dot(jnp.concatenate([mixed[start : start + HEAD], ones], axis=0), powers)
        share = 1.0 / sums[HEAD : HEAD + 1]
        outs.append(sums[:HEAD] * share)
        shares.append(share)
    return jnp.concatenate(outs, axis=0).astype(bf16), jnp.concatenate(shares, axis=0)


def attend_back(mixed, attended, gradient, shares, width, powers_ref, first_power):
    keys = turned(mixed[width : 2 * width])
    values = turned(mixed[2 * width :])
    grad_queries, grad_keys, grad_values = [], [], []
    for group in range(0, width // HEAD, 4):
        spreads = []
        for head in range(group, group + 4):
            part = slice(HEAD * head, HEAD * (head + 1))
            shared = gradient[part] * shares[head : head + 1]
            overlap = jnp.sum(shared * attended[part].astype(f32), axis=0, keepdims=True)
            shared = shared.astype(bf16)
            spreads.append((dot(values, padded(shared, head, width)), overlap))
            grad_values.append(dot_nt(shared, powers_ref[first_power + head]))
        for head in range(group, group + 4):
            spread, overlap = spreads[head - group]
            powers = powers_ref[first_power + head].astype(f32)
            change = (powers * (spread - overlap)).astype(bf16)
            key_rows = mixed[width + HEAD * head : width + HEAD * (head + 1)]
            grad_queries.append(dot(key_rows, change) * HEAD**-0.5)
            grad_keys.append(dot_nt(mixed[HEAD * head : HEAD * (head + 1)], change) * HEAD**-0.5)
    return jnp.concatenate(grad_queries + grad_keys + grad_values, axis=0).astype(bf16)


def block_front(inputs, inlet_t, outlet_t, widen_t, narrow_t, powers_ref, first_power):
    width = inputs.shape[0]
    start = inputs.astype(f32)
    normed = norm(start)[0].astype(bf16)
    mixed = dot(inlet_t, normed).astype(bf16)
    attended, shares = attend(mixed, width, powers_ref, first_power)
    middle = start + dot(outlet_t, attended)
    second = norm(middle)[0].astype(bf16)
    values = dot(widen_t, second)
    below = 0.5 + 0.5 * lax.erf(values * math.sqrt(0.5))
    hidden = (values * below).astype(bf16)
    result = (middle + dot(narrow_t, hidden)).astype(bf16)
    return result, mixed, attended, shares, hidden, values, below


def gelu_slope(values, below):
    bell = jnp.exp(-0.5 * values * values) * (1.0 / math.sqrt(2.0 * math.pi))
    return (below + values * bell).astype(bf16)


def norms(inputs, attended, outlet_t):
    start = inputs.astype(f32)
    return norm(start) + norm(start + dot(outlet_t, attended))


def block_back(prepared, mixed, attended, shares, hidden, slope, gradient, weights, powers_ref, first_power):
    inlet, outlet, widen, narrow = weights
    normed, rate, second, rate_two = prepared
    width = normed.shape[0]
    grad_wide = (dot(narrow, gradient) * slope.astype(f32)).astype(bf16)
    grad_middle = gradient.astype(f32) + norm_back(dot(widen, grad_wide), second, rate_two)
    short = grad_middle.astype(bf16)
    grad_mixed = attend_back(mixed, attended, dot(outlet, short), shares, width, powers_ref, first_power)
    grad_inputs = grad_middle + norm_back(dot(inlet, grad_mixed), normed, rate)

    def weight_grads():
        return (
            dot_nt(normed.astype(bf16), grad_mixed),
            dot_nt(attended, short),
            dot_nt(second.astype(bf16), grad_wide),
            dot_nt(gradient, hidden),
        )

    return grad_inputs.astype(bf16), weight_grads


def ranks(owner):
    before_me = jnp.where(rows_of(256, 256) < lax.broadcasted_iota(i32, (256, 256), 1), 1.0, 0.0)
    before_me = before_me.astype(bf16)
    before = jnp.zeros((PEERS, 1), f32)
    found = []
    for start in range(0, owner.shape[1], 256):
        hits = jnp.where(rows_of(PEERS, 256) == owner[:, start : start + 256], 1.0, 0.0)
        count = dot(hits.astype(bf16), before_me) + before
        found.append(jnp.sum(hits * count, axis=0, keepdims=True))
        before = before + jnp.sum(hits, axis=1, keepdims=True)
    return jnp.concatenate(found, axis=1).astype(i32)


def marks(owner, rank, value):
    hits = match(owner, PEERS)
    at = rows_of(128, owner.shape[1]) == rank
    high = jnp.where(at, (value >> 6).astype(f32), 0.0).astype(bf16)
    low = jnp.where(at, (value & 63).astype(f32), 0.0).astype(bf16)
    return dot_nt(hits, high) * 64.0 + dot_nt(hits, low)


def spread_places(table):
    lane = lax.broadcasted_iota(i32, (PEERS, 128), 1)
    apart = table + jnp.where(lane >= 64, 4096.0, 0.0)
    over = jnp.zeros((PEERS, 128), f32)
    for shift in range(1, 64):
        over = jnp.where(apart == pltpu.roll(apart, 128 - shift, 1), 1.0, over)
    high = jnp.floor(table * (1.0 / 64.0))
    low = table - 64.0 * high
    high = high + 64.0 * over
    stack = []
    for part in range(5):
        stack += [high[:, 16 * part : 16 * part + 16], low[:, 16 * part : 16 * part + 16]]
    stack = jnp.concatenate(stack, axis=0).astype(bf16)
    column = lax.broadcasted_iota(i32, (16, 1024), 1)
    spread = dot(stack, jnp.where(column % 16 == rows_of(16, 1024), 1.0, 0.0).astype(bf16))
    own = rows_of(PEERS, 1024) == lax.broadcasted_iota(i32, (PEERS, 1024), 1) // 16
    places, drops = [], []
    for part in range(5):
        high = jnp.sum(jnp.where(own, spread[128 * part : 128 * part + 64], 0.0), axis=0, keepdims=True)
        low = jnp.sum(jnp.where(own, spread[128 * part + 64 : 128 * part + 128], 0.0), axis=0, keepdims=True)
        drops.append(high > 63.5)
        high = jnp.where(high > 63.5, high - 64.0, high)
        places.append((high * 64.0 + low).astype(i32) - 1)
    return places, drops


def last_senders(inside, hits):
    width = hits[0].shape[0]
    count = len(inside[0])
    sender = lax.broadcasted_iota(i32, (1, 1024), 1) // 16
    own = rows_of(PEERS, 1024) == sender
    seen = jnp.zeros((PEERS * count, width), f32)
    for masks, hit in zip(inside, hits):
        wide = [jnp.where(own & mask, 1.0, 0.0) for mask in masks]
        seen += dot_nt(jnp.concatenate(wide, axis=0).astype(bf16), hit)
    index = rows_of(PEERS, width).astype(f32)
    lasts = []
    for part in range(count):
        lasts.append(jnp.max(jnp.where(seen[PEERS * part : PEERS * part + PEERS] > 0.5, index, -1.0), axis=0, keepdims=True))
    lasts = jnp.concatenate(lasts + [jnp.zeros((16 - count, width), f32)], axis=0).astype(bf16)
    found = []
    for masks, hit in zip(inside, hits):
        got = dot(lasts, hit)
        mine = jnp.full((1, 1024), -1.0, f32)
        for part in range(count):
            mine = jnp.where(masks[part], got[part : part + 1], mine)
        found.append(mine == sender.astype(f32))
    return found


def greet_peers(me):
    barrier = pltpu.get_barrier_semaphore()

    def greet(step, carry):
        pl.semaphore_signal(
            barrier, device_id={"pts": (me + step) % PEERS}, device_id_type=MESH
        )
        return carry

    lax.fori_loop(1, PEERS, greet, 0)
    return barrier


def send_to(source, target, sems, index, device):
    return pltpu.make_async_remote_copy(
        source, target, sems.at[index], sems.at[index + 1], device_id=device, device_id_type=MESH
    )


def batch_of(me, target, count, sems, index):
    some = target.at[pl.ds(0, count - 1)]
    return send_to(some, some, sems, index, {"pts": me})


def exchange(me, source, target, sems, index):

    def send(step, carry):
        along, across = step // 8, step // 2 % 4
        z = (me // 8 + 4 + (along + 1) // 2 * (1 - along % 2 * 2)) % 8
        y = (me // 2 + 2 + (across + 1) // 2 * (1 - across % 2 * 2)) % 4
        other = z * 8 + y * 2 + (me + 1 + step) % 2
        send_to(source.at[other], target.at[me], sems, index, {"pts": other}).start()
        return carry

    lax.fori_loop(0, PEERS - 1, send, 0)
    target[me] = source[me]
    return batch_of(me, target, PEERS, sems, index)


def exchange_parts(me, make_part, source, target, sems, index):
    for turn in range(4):
        quarter = (me // 16 + turn) % 4
        source[pl.ds(16 * quarter, 16)] = make_part(quarter)

        def send(step, carry, quarter=quarter):
            other = 16 * quarter + (me + step) % 16
            send_to(source.at[other], target.at[me], sems, index, {"pts": other}).start()
            return carry

        lax.fori_loop(1 if turn == 0 else 0, 16, send, 0)
    target[me] = source[me]
    return batch_of(me, target, PEERS, sems, index)


class Adder:
    def __init__(self, scale, half, near, part, far, near_out, out, sems, index):
        self.scale, self.half, self.near, self.part, self.far = scale, half, near, part, far
        self.near_out, self.out, self.sems, self.index = near_out, out, sems, index
        self.me, rep = lax.axis_index("pts"), lax.axis_index("rep")
        self.inside, self.layer = self.me % 8, self.me // 8
        self.mine = self.inside * 4 + rep

    def near_device(self, step):
        other = (self.mine + step) % NEAR
        return other, {"pts": self.layer * 8 + other // 4, "rep": other % 4}

    def far_device(self, step):
        other = (self.layer + step) % FAR
        return other, {"pts": other * 8 + self.inside}

    def batch(self, target, count, stage):
        return batch_of(self.me, target, count, self.sems, self.index + 2 * stage)

    def loop(self, count, source_of, target, stage, device_of):
        def send(step, carry):
            other, device = device_of(step)
            send_to(source_of(other), target, self.sems, self.index + 2 * stage, device).start()
            return carry

        lax.fori_loop(1, count, send, 0)

    def send_near(self):
        self.loop(NEAR, lambda other: self.half.at[other], self.near.at[self.mine], 0, self.near_device)
        self.near[self.mine] = self.half[self.mine]

    def send_far(self):
        self.batch(self.near, NEAR, 0).wait_recv()
        total = self.near[0].astype(f32)
        for index in range(1, NEAR):
            total = total + self.near[index].astype(f32)
        self.part[...] = total.astype(bf16)
        self.loop(FAR, lambda other: self.part, self.far.at[self.layer], 1, self.far_device)
        self.far[self.layer] = self.part[...]

    def spread_near(self):
        self.batch(self.far, FAR, 1).wait_recv()
        total = self.far[0].astype(f32)
        for index in range(1, FAR):
            total = total + self.far[index].astype(f32)
        self.near_out[...] = (total * self.scale).astype(bf16)
        self.loop(NEAR, lambda other: self.near_out, self.out.at[self.mine], 2, self.near_device)
        self.out[self.mine] = self.near_out[...]

    def end(self):
        self.batch(self.out, NEAR, 2).wait_recv()
        self.batch(self.near, NEAR, 0).wait_send()
        self.batch(self.far, FAR, 1).wait_send()
        self.batch(self.out, NEAR, 2).wait_send()


def adder_scratch(rows):
    return [
        pltpu.VMEM((NEAR, rows, 128), bf16),
        pltpu.VMEM((NEAR, rows, 128), bf16),
        pltpu.VMEM((rows, 128), bf16),
        pltpu.VMEM((FAR, rows, 128), bf16),
        pltpu.VMEM((rows, 128), bf16),
    ]


def store_lanes(ref, row, array):
    height, block = array.shape[0], ref.shape[1]
    for index in range(array.shape[1] // 128):
        part = array[:, 128 * index : 128 * index + 128].astype(ref.dtype)
        start, done = row + height * index, 0
        while done < height:
            count = min(height - done, block - (start + done) % block)
            inside = (start + done) % block
            ref[(start + done) // block, inside : inside + count, :] = part[done : done + count]
            done += count


def load_lanes(ref, row, height, count):
    parts = [ref[row + height * index : row + height * (index + 1), :].astype(f32) for index in range(count)]
    return jnp.concatenate(parts, axis=1) if count > 1 else parts[0]


def main_kernel(
    scale,
    feats_ref, first_ref, ident_ref, second_ref, cotangent_ref,
    inlet_one, outlet_one, widen_one, narrow_one_t, pool_ref, inlet_two, outlet_two, widen_two, narrow_two,
    second_out, feats_out, sums_one, sums_two,
    mark, marks_in, send_one, rows_one, send_two, rows_two, send_three, rows_three, send_four, rows_four,
    places_ref, hits_ref, member_ref, taking_ref, inputs_ref, mixed_ref, attended_ref, shares_ref, hidden_ref,
    values_ref, below_ref, slope_ref, normed_ref, norm_two_ref, rates_ref, powers_one, powers_two, *rest,
):
    me = lax.axis_index("pts")
    sems = rest[-1]
    late = Adder(scale, *rest[:5], sums_one, sems, 10)
    early = Adder(scale, *rest[5:10], sums_two, sems, 16)
    barrier = greet_peers(me)

    def greet_near(step, carry):
        pl.semaphore_signal(barrier, device_id=early.near_device(step)[1], device_id_type=MESH)
        return carry

    lax.fori_loop(1, NEAR, greet_near, 0)

    first, second = first_ref[...], second_ref[...]
    owner_one, owner_two = first // ROWS, second // COARSE
    rank_one, rank_two = ranks(owner_one), ranks(owner_two)
    slot_one, layer_one = owner_one * 16 + rank_one % 16, rank_one // 16
    feats = feats_ref[...].astype(f32)
    wide = [jnp.where(layer_one == index, feats, 0.0) for index in range(4)]
    wide = jnp.concatenate(wide, axis=0).astype(bf16)
    for part in range(4):
        packed = dot_nt(match(slot_one - 256 * part, 256), wide).astype(bf16)
        send_one[16 * part : 16 * part + 16] = packed.reshape(16, 16, 256)
    found = marks(owner_one, rank_one, first % ROWS + 1)
    found += marks(owner_two, rank_two + 64, second % COARSE + 1)
    mark[:, 0, :] = found
    taking_ref[...] = match(owner_two * 16 + rank_two, 1024)
    for patch in range(PATCHES):
        member_ref[patch] = match(ident_ref[:, patch * PATCH : (patch + 1) * PATCH], COARSE)
    pl.semaphore_wait(barrier, PEERS + NEAR - 2)
    marked = exchange(me, mark, marks_in, sems, 0)
    moved_one = exchange(me, send_one, rows_one, sems, 2)

    weights_one = [inlet_one[...], outlet_one[...], widen_one[...], turned(narrow_one_t[...])]
    turned_one = [turned(weight) for weight in weights_one[:3]] + [narrow_one_t[...]]
    marked.wait_recv()
    places, drops = spread_places(marks_in[:, 0, :])
    for part in range(5):
        places_ref[part : part + 1, :] = places[part]
    kept = [jnp.where(drop, -1, place) for place, drop in zip(places, drops)]
    for layer in range(4):
        hits_ref[layer] = match(places[layer] % 512, 512)
    hits = [hits_ref[layer] for layer in range(4)]
    last = last_senders([[place // 512 == patch for patch in range(PATCHES)] for place in kept[:4]], hits)
    last_two = last_senders([[kept[4] >= 0]], [match(kept[4], COARSE)])
    places_ref[5:6, :] = jnp.where(last_two[0], kept[4], -1)
    moved_one.wait_recv()
    arrived = rows_one[...].reshape(1024, 256).astype(f32).T
    landed = jnp.zeros((256, 512), f32)
    for layer in range(4):
        place = jnp.where(last[layer], kept[layer], -1)
        points = arrived[64 * layer : 64 * layer + 64]
        spread = [jnp.where(place // 512 == patch, points, 0.0) for patch in range(PATCHES)]
        landed += dot_nt(jnp.concatenate(spread, axis=0).astype(bf16), hits[layer])
    inputs_ref[...] = landed.astype(bf16).reshape(PATCHES, 64, PATCH)
    total = jnp.zeros((80, COARSE), f32)
    for patch in range(PATCHES):
        result, mixed, attended, shares, hidden, values, below = block_front(
            inputs_ref[patch], *turned_one, powers_one, 4 * patch
        )
        mixed_ref[patch] = mixed
        attended_ref[patch] = attended
        shares_ref[patch] = shares
        hidden_ref[patch] = hidden
        values_ref[patch] = values
        below_ref[patch] = below
        counted = jnp.concatenate([result, jnp.ones((16, PATCH), bf16)], axis=0)
        total += dot_nt(counted, member_ref[patch])
    sizes = total[64:65]
    pooled = (total[:64] / sizes).astype(bf16)
    coarse = dot(turned(pool_ref[...]), pooled).astype(bf16)
    send_two[...] = dot_nt(taking_ref[...], coarse).astype(bf16).reshape(PEERS, 16, 128)
    moved_two = exchange(me, send_two, rows_two, sems, 4)

    def slopes(patch, carry):
        slope_ref[patch] = gelu_slope(values_ref[patch], below_ref[patch])
        return carry

    lax.fori_loop(0, PATCHES, slopes, 0)
    weights_two = [inlet_two[...], outlet_two[...], widen_two[...], narrow_two[...]]
    turned_two = [turned(weight) for weight in weights_two]
    gradient = turned(cotangent_ref[...])
    landing = match(places_ref[5:6, :], COARSE)
    for patch in range(PATCHES):
        normed, rate, second, rate_two = norms(inputs_ref[patch], attended_ref[patch], turned_one[1])
        normed_ref[patch] = normed
        norm_two_ref[patch] = second
        rates_ref[patch] = jnp.concatenate([rate, rate_two], axis=0)
    moved_two.wait_recv()

    inputs = dot_nt(turned(rows_two[...].reshape(1024, 128)), landing).astype(bf16)
    result, mixed, attended, shares, hidden, values, below = block_front(inputs, *turned_two, powers_two, 0)
    back, grads_of = block_back(
        norms(inputs, attended, turned_two[1]), mixed, attended, shares, hidden, gelu_slope(values, below), gradient,
        weights_two, powers_two, 0,
    )
    send_three[...] = turned(dot(back, match(places_ref[4:5, :], COARSE))).reshape(PEERS, 16, 128)
    moved_three = exchange(me, send_three, rows_three, sems, 6)
    row = 0
    for grad in grads_of():
        store_lanes(early.half, row, grad)
        row += grad.shape[0] * grad.shape[1] // 128
    early.send_near()
    second_out[...] = turned(result)
    moved_three.wait_recv()

    grad_coarse = dot(turned(rows_three[...].reshape(1024, 128)), taking_ref[...]).astype(bf16)
    grad_pool = dot_nt(pooled, grad_coarse)
    grad_pooled = dot(pool_ref[...], grad_coarse).astype(bf16).astype(f32)
    share = (grad_pooled / sizes).astype(bf16)

    backs, front_total, widen_total, narrow_total = [], 0.0, 0.0, 0.0
    for patch in range(PATCHES):
        gradient = dot(share, member_ref[patch]).astype(bf16)
        prepared = normed_ref[patch], rates_ref[patch, 0:1], norm_two_ref[patch], rates_ref[patch, 1:2]
        back, grads_of = block_back(
            prepared, mixed_ref[patch], attended_ref[patch], shares_ref[patch], hidden_ref[patch],
            slope_ref[patch], gradient, weights_one, powers_one, 4 * patch,
        )
        backs.append(back)
        grad_inlet, grad_outlet, grad_widen, grad_narrow = grads_of()
        front_total += jnp.concatenate([grad_inlet, grad_outlet], axis=1)
        widen_total += grad_widen
        narrow_total += grad_narrow
        if patch == 0:
            early.send_far()
        if patch == 2:
            early.spread_near()
    store_lanes(late.half, 0, front_total)
    store_lanes(late.half, 128, widen_total)
    store_lanes(late.half, 256, narrow_total)
    store_lanes(late.half, 384, grad_pool)
    late.half[28:] = jnp.zeros((4, 16, 128), bf16)
    late.send_near()
    back = jnp.concatenate(backs, axis=0)

    def take(quarter):
        taken = []
        for layer in range(4):
            place = places_ref[layer : layer + 1, pl.ds(pl.multiple_of(quarter * 256, 256), 256)]
            found = dot(back, hits_ref[layer, :, pl.ds(pl.multiple_of(quarter * 256, 256), 256)])
            parts = [
                jnp.where(place // 512 == patch, found[64 * patch : 64 * patch + 64], 0.0) for patch in range(PATCHES)
            ]
            taken.append(parts[0] + parts[1] + parts[2] + parts[3])
        return jnp.concatenate(taken, axis=0).T.astype(bf16).reshape(16, 16, 256)

    moved_four = exchange_parts(me, take, send_four, rows_four, sems, 8)
    late.send_far()
    picking = match(slot_one, 1024)
    late.spread_near()
    moved_four.wait_recv()
    found = dot(turned(rows_four[...].reshape(1024, 256)), picking)
    parts = [jnp.where(layer_one == index, found[64 * index : 64 * index + 64], 0.0) for index in range(4)]
    feats_out[...] = (parts[0] + parts[1] + parts[2] + parts[3]).astype(bf16)
    early.end()
    late.end()
    marked.wait_send()
    moved_one.wait_send()
    moved_two.wait_send()
    moved_three.wait_send()
    moved_four.wait_send()


def output_kernel(
    second_in, feats_in, late_ref, early_ref,
    second_out, feats_out, inlet_one, outlet_one, widen_one, narrow_one_t, pool,
    inlet_two, outlet_two, widen_two, narrow_two,
):
    second_out[...] = second_in[...]
    feats_out[...] = feats_in[...]
    front = load_lanes(late_ref, 0, 64, 2)
    inlet_one[...] = front[:, :192]
    outlet_one[...] = front[:, 192:]
    widen_one[...] = load_lanes(late_ref, 128, 64, 2)
    narrow_one_t[...] = load_lanes(late_ref, 256, 64, 2)
    pool[...] = load_lanes(late_ref, 384, 64, 1)
    inlet_two[...] = load_lanes(early_ref, 0, 128, 3)
    outlet_two[...] = load_lanes(early_ref, 384, 128, 1)
    widen_two[...] = load_lanes(early_ref, 512, 128, 4)
    narrow_two[...] = load_lanes(early_ref, 1024, 128, 4).T


def call(kernel, outs, scratch, *operands, collective=None):
    params = {} if collective is None else {"collective_id": collective, "has_side_effects": True}
    whole = pl.BlockSpec(memory_space=pltpu.VMEM)
    return pl.pallas_call(
        kernel,
        out_shape=[jax.ShapeDtypeStruct(shape, dtype) for shape, dtype in outs],
        in_specs=[whole] * len(operands),
        out_specs=[whole] * len(outs),
        scratch_shapes=scratch,
        compiler_params=pltpu.CompilerParams(vmem_limit_bytes=56 * 2**20, **params),
    )(*operands)


def shards(
    feats,
    dest_first,
    pool_ids,
    dest_second,
    cotangent,
    inlet_first,
    outlet_first,
    widen_first,
    narrow_first,
    pool_weight,
    inlet_second,
    outlet_second,
    widen_second,
    narrow_second,
):
    scale = 1.0 / math.sqrt(lax.axis_size("rep") * lax.axis_size("pts") * COARSE)
    wide_slots, slots = pltpu.VMEM((PEERS, 16, 256), bf16), pltpu.VMEM((PEERS, 16, 128), bf16)
    mark = pltpu.VMEM((PEERS, 1, 128), f32)
    moved = call(
        lambda *refs: main_kernel(scale, *refs),
        [((COARSE, 128), bf16), ((64, ROWS), bf16), ((NEAR, 16, 128), bf16), ((NEAR, 48, 128), bf16)],
        [mark, mark, wide_slots, wide_slots, slots, slots, slots, slots, wide_slots, wide_slots]
        + [
            pltpu.VMEM((6, 1024), i32),
            pltpu.VMEM((4, 512, 1024), bf16),
            pltpu.VMEM((PATCHES, COARSE, PATCH), bf16),
            pltpu.VMEM((1024, COARSE), bf16),
            pltpu.VMEM((PATCHES, 64, PATCH), bf16),
            pltpu.VMEM((PATCHES, 192, PATCH), bf16),
            pltpu.VMEM((PATCHES, 64, PATCH), bf16),
            pltpu.VMEM((PATCHES, 4, PATCH), f32),
            pltpu.VMEM((PATCHES, 256, PATCH), bf16),
            pltpu.VMEM((PATCHES, 256, PATCH), f32),
            pltpu.VMEM((PATCHES, 256, PATCH), f32),
            pltpu.VMEM((PATCHES, 256, PATCH), bf16),
            pltpu.VMEM((PATCHES, 64, PATCH), f32),
            pltpu.VMEM((PATCHES, 64, PATCH), f32),
            pltpu.VMEM((PATCHES, 2, PATCH), f32),
            pltpu.VMEM((16, PATCH, PATCH), bf16),
            pltpu.VMEM((8, PATCH, PATCH), bf16),
        ]
        + adder_scratch(16)
        + adder_scratch(48)
        + [pltpu.SemaphoreType.DMA((22,))],
        feats[0].T, dest_first, pool_ids, dest_second, cotangent[0],
        inlet_first, outlet_first, widen_first, narrow_first.T, pool_weight,
        inlet_second, outlet_second, widen_second, narrow_second,
        collective=1,
    )
    second_out, feats_grad, late, early = moved
    weights = (inlet_first, outlet_first, widen_first, narrow_first.T, pool_weight)
    weights += (inlet_second, outlet_second, widen_second, narrow_second)
    second_out, feats_grad, *totals = call(
        output_kernel,
        [((COARSE, 128), bf16), ((64, ROWS), bf16)] + [(weight.shape, f32) for weight in weights],
        [],
        second_out, feats_grad, late.reshape(512, 128), early.reshape(1536, 128),
    )
    totals[3] = totals[3].T
    return (second_out[None], feats_grad.T[None], *totals)


def solution(mesh):
    split = P("rep", "pts")
    return jax.shard_map(
        shards,
        mesh=mesh,
        in_specs=(split,) * 5 + (P(),) * 9,
        out_specs=(split,) * 2 + (P(),) * 9,
        check_vma=False,
    )
```

```python
import math

import jax
import jax.numpy as jnp
from jax import lax
from jax.experimental import pallas as pl
from jax.experimental.pallas import tpu as pltpu
from jax.sharding import PartitionSpec as P


HEAD = 16
PATCH = 512
PATCHES = 4
ROWS = 2048
COARSE = 512
PEERS = 64
NEAR, FAR = 32, 8
MESH = pl.DeviceIdType.MESH
SHARPEN = HEAD**-0.5 / math.log(2.0)
f32, bf16, i32 = jnp.float32, jnp.bfloat16, jnp.int32


def dot(left, right):
    return jnp.dot(left, right, preferred_element_type=f32)


def dot_nt(left, right):
    return lax.dot_general(left, right, (((1,), (1,)), ((), ())), preferred_element_type=f32)


def turned(array):
    return array.astype(f32).T.astype(bf16)


def rows_of(count, width):
    return lax.broadcasted_iota(i32, (count, width), 0)


def match(row, count):
    return jnp.where(rows_of(count, row.shape[1]) == row, 1.0, 0.0).astype(bf16)


def norm(values):
    centred = values - jnp.mean(values, axis=0, keepdims=True)
    rate = lax.rsqrt(jnp.mean(centred * centred, axis=0, keepdims=True) + 1e-05)
    return centred * rate, rate


def norm_back(gradient, normed, rate):
    mean = jnp.mean(gradient, axis=0, keepdims=True)
    along = jnp.mean(gradient * normed, axis=0, keepdims=True)
    return rate * (gradient - mean - normed * along)


def padded(rows, head, width):
    parts = [rows]
    if head > 0:
        parts.insert(0, jnp.zeros((HEAD * head, rows.shape[1]), rows.dtype))
    rest = width - HEAD * (head + 1)
    if rest > 0:
        parts.append(jnp.zeros((rest, rows.shape[1]), rows.dtype))
    return jnp.concatenate(parts, axis=0)


def only(array, head):
    return padded(array[HEAD * head : HEAD * (head + 1)], head, array.shape[0])


def attend(mixed, width, powers_ref, first_power):
    keys = turned(mixed[width : 2 * width])
    ones = jnp.ones((HEAD, PATCH), bf16)
    outs, shares = [], []
    later = dot(keys, only(mixed[:width], 0))
    for head in range(width // HEAD):
        scores = later
        if head + 1 < width // HEAD:
            later = dot(keys, only(mixed[:width], head + 1))
        top = jnp.max(scores, axis=0, keepdims=True)
        powers = jnp.exp2((scores - top) * SHARPEN).astype(bf16)
        powers_ref[first_power + head] = powers
        start = 2 * width + HEAD * head
        sums = dot(jnp.concatenate([mixed[start : start + HEAD], ones], axis=0), powers)
        share = 1.0 / sums[HEAD : HEAD + 1]
        outs.append(sums[:HEAD] * share)
        shares.append(share)
    return jnp.concatenate(outs, axis=0).astype(bf16), jnp.concatenate(shares, axis=0)


def attend_back(mixed, attended, gradient, shares, width, powers_ref, first_power):
    keys = turned(mixed[width : 2 * width])
    values = turned(mixed[2 * width :])
    grad_queries, grad_keys, grad_values = [], [], []
    for group in range(0, width // HEAD, 4):
        spreads = []
        for head in range(group, group + 4):
            part = slice(HEAD * head, HEAD * (head + 1))
            shared = gradient[part] * shares[head : head + 1]
            overlap = jnp.sum(shared * attended[part].astype(f32), axis=0, keepdims=True)
            shared = shared.astype(bf16)
            spreads.append((dot(values, padded(shared, head, width)), overlap))
            grad_values.append(dot_nt(shared, powers_ref[first_power + head]))
        for head in range(group, group + 4):
            spread, overlap = spreads[head - group]
            powers = powers_ref[first_power + head].astype(f32)
            change = (powers * (spread - overlap)).astype(bf16)
            key_rows = mixed[width + HEAD * head : width + HEAD * (head + 1)]
            grad_queries.append(dot(key_rows, change) * HEAD**-0.5)
            grad_keys.append(dot_nt(mixed[HEAD * head : HEAD * (head + 1)], change) * HEAD**-0.5)
    return jnp.concatenate(grad_queries + grad_keys + grad_values, axis=0).astype(bf16)


def block_front(inputs, inlet_t, outlet_t, widen_t, narrow_t, powers_ref, first_power):
    width = inputs.shape[0]
    start = inputs.astype(f32)
    normed = norm(start)[0].astype(bf16)
    mixed = dot(inlet_t, normed).astype(bf16)
    attended, shares = attend(mixed, width, powers_ref, first_power)
    middle = start + dot(outlet_t, attended)
    second = norm(middle)[0].astype(bf16)
    values = dot(widen_t, second)
    hidden = (values * gelu_below(values)).astype(bf16)
    result = (middle + dot(narrow_t, hidden)).astype(bf16)
    return result, mixed, attended, shares, hidden, values


def gelu_below(values):
    return 0.5 + 0.5 * lax.erf(values * math.sqrt(0.5))


def gelu_slope(values):
    bell = jnp.exp(-0.5 * values * values) * (1.0 / math.sqrt(2.0 * math.pi))
    return (gelu_below(values) + values * bell).astype(bf16)


def norms(inputs, attended, outlet_t):
    start = inputs.astype(f32)
    return norm(start) + norm(start + dot(outlet_t, attended))


def block_back(prepared, mixed, attended, shares, hidden, slope, gradient, weights, powers_ref, first_power):
    inlet, outlet, widen, narrow = weights
    normed, rate, second, rate_two = prepared
    width = normed.shape[0]
    grad_wide = (dot(narrow, gradient) * slope.astype(f32)).astype(bf16)
    grad_middle = gradient.astype(f32) + norm_back(dot(widen, grad_wide), second, rate_two)
    short = grad_middle.astype(bf16)
    grad_mixed = attend_back(mixed, attended, dot(outlet, short), shares, width, powers_ref, first_power)
    grad_inputs = grad_middle + norm_back(dot(inlet, grad_mixed), normed, rate)

    def weight_grads():
        return (
            dot_nt(normed.astype(bf16), grad_mixed),
            dot_nt(attended, short),
            dot_nt(second.astype(bf16), grad_wide),
            dot_nt(gradient, hidden),
        )

    return grad_inputs.astype(bf16), weight_grads


def ranks(owner):
    before_me = jnp.where(rows_of(256, 256) < lax.broadcasted_iota(i32, (256, 256), 1), 1.0, 0.0)
    before_me = before_me.astype(bf16)
    before = jnp.zeros((PEERS, 1), f32)
    found = []
    for start in range(0, owner.shape[1], 256):
        hits = jnp.where(rows_of(PEERS, 256) == owner[:, start : start + 256], 1.0, 0.0)
        count = dot(hits.astype(bf16), before_me) + before
        found.append(jnp.sum(hits * count, axis=0, keepdims=True))
        before = before + jnp.sum(hits, axis=1, keepdims=True)
    return jnp.concatenate(found, axis=1).astype(i32)


def marks(owner, rank, value):
    hits = match(owner, PEERS)
    at = rows_of(128, owner.shape[1]) == rank
    high = jnp.where(at, (value >> 6).astype(f32), 0.0).astype(bf16)
    low = jnp.where(at, (value & 63).astype(f32), 0.0).astype(bf16)
    return dot_nt(hits, high) * 64.0 + dot_nt(hits, low)


def spread_places(table):
    lane = lax.broadcasted_iota(i32, (PEERS, 128), 1)
    apart = table + jnp.where(lane >= 64, 4096.0, 0.0)
    over = jnp.zeros((PEERS, 128), f32)
    for shift in range(1, 64):
        over = jnp.where(apart == pltpu.roll(apart, 128 - shift, 1), 1.0, over)
    high = jnp.floor(table * (1.0 / 64.0))
    low = table - 64.0 * high
    high = high + 64.0 * over
    stack = []
    for part in range(5):
        stack += [high[:, 16 * part : 16 * part + 16], low[:, 16 * part : 16 * part + 16]]
    stack = jnp.concatenate(stack, axis=0).astype(bf16)
    column = lax.broadcasted_iota(i32, (16, 1024), 1)
    spread = dot(stack, jnp.where(column % 16 == rows_of(16, 1024), 1.0, 0.0).astype(bf16))
    own = rows_of(PEERS, 1024) == lax.broadcasted_iota(i32, (PEERS, 1024), 1) // 16
    places, drops = [], []
    for part in range(5):
        high = jnp.sum(jnp.where(own, spread[128 * part : 128 * part + 64], 0.0), axis=0, keepdims=True)
        low = jnp.sum(jnp.where(own, spread[128 * part + 64 : 128 * part + 128], 0.0), axis=0, keepdims=True)
        drops.append(high > 63.5)
        high = jnp.where(high > 63.5, high - 64.0, high)
        places.append((high * 64.0 + low).astype(i32) - 1)
    return places, drops


def last_senders(inside, hits):
    width = hits[0].shape[0]
    count = len(inside[0])
    sender = lax.broadcasted_iota(i32, (1, 1024), 1) // 16
    own = rows_of(PEERS, 1024) == sender
    seen = jnp.zeros((PEERS * count, width), f32)
    for masks, hit in zip(inside, hits):
        wide = [jnp.where(own & mask, 1.0, 0.0) for mask in masks]
        seen += dot_nt(jnp.concatenate(wide, axis=0).astype(bf16), hit)
    index = rows_of(PEERS, width).astype(f32)
    lasts = []
    for part in range(count):
        lasts.append(jnp.max(jnp.where(seen[PEERS * part : PEERS * part + PEERS] > 0.5, index, -1.0), axis=0, keepdims=True))
    lasts = jnp.concatenate(lasts + [jnp.zeros((16 - count, width), f32)], axis=0).astype(bf16)
    found = []
    for masks, hit in zip(inside, hits):
        got = dot(lasts, hit)
        mine = jnp.full((1, 1024), -1.0, f32)
        for part in range(count):
            mine = jnp.where(masks[part], got[part : part + 1], mine)
        found.append(mine == sender.astype(f32))
    return found


def greet_peers(me):
    barrier = pltpu.get_barrier_semaphore()

    def greet(step, carry):
        pl.semaphore_signal(
            barrier, device_id={"pts": (me + step) % PEERS}, device_id_type=MESH
        )
        return carry

    lax.fori_loop(1, PEERS, greet, 0)
    return barrier


def send_to(source, target, sems, index, device):
    return pltpu.make_async_remote_copy(
        source, target, sems.at[index], sems.at[index + 1], device_id=device, device_id_type=MESH
    )


def batch_of(me, target, count, sems, index):
    some = target.at[pl.ds(0, count - 1)]
    return send_to(some, some, sems, index, {"pts": me})


def exchange(me, source, target, sems, index):

    def send(step, carry):
        along, across = step // 8, step // 2 % 4
        z = (me // 8 + 4 + (along + 1) // 2 * (1 - along % 2 * 2)) % 8
        y = (me // 2 + 2 + (across + 1) // 2 * (1 - across % 2 * 2)) % 4
        other = z * 8 + y * 2 + (me + 1 + step) % 2
        send_to(source.at[other], target.at[me], sems, index, {"pts": other}).start()
        return carry

    lax.fori_loop(0, PEERS - 1, send, 0)
    target[me] = source[me]
    return batch_of(me, target, PEERS, sems, index)


def exchange_parts(me, make_part, between, source, target, sems, index):
    for turn in (2, 1, 3, 0):
        quarter = (me // 16 + turn) % 4
        source[pl.ds(16 * quarter, 16)] = make_part(quarter)

        def send(step, carry, quarter=quarter):
            other = 16 * quarter + (me + step) % 16
            send_to(source.at[other], target.at[me], sems, index, {"pts": other}).start()
            return carry

        lax.fori_loop(1 if turn == 0 else 0, 16, send, 0)
        if turn == 1:
            between()
    target[me] = source[me]
    return batch_of(me, target, PEERS, sems, index)


class Adder:
    def __init__(self, scale, half, near, part, far, near_out, out, sems, index):
        self.scale, self.half, self.near, self.part, self.far = scale, half, near, part, far
        self.near_out, self.out, self.sems, self.index = near_out, out, sems, index
        self.me, rep = lax.axis_index("pts"), lax.axis_index("rep")
        self.inside, self.layer = self.me % 8, self.me // 8
        self.mine = self.inside * 4 + rep

    def near_device(self, step):
        other = (self.mine + step) % NEAR
        return other, {"pts": self.layer * 8 + other // 4, "rep": other % 4}

    def far_device(self, step):
        other = (self.layer + step) % FAR
        return other, {"pts": other * 8 + self.inside}

    def batch(self, target, count, stage):
        return batch_of(self.me, target, count, self.sems, self.index + 2 * stage)

    def loop(self, count, source_of, target, stage, device_of):
        def send(step, carry):
            other, device = device_of(step)
            send_to(source_of(other), target, self.sems, self.index + 2 * stage, device).start()
            return carry

        lax.fori_loop(1, count, send, 0)

    def send_near(self):
        self.loop(NEAR, lambda other: self.half.at[other], self.near.at[self.mine], 0, self.near_device)
        self.near[self.mine] = self.half[self.mine]

    def send_far(self):
        self.batch(self.near, NEAR, 0).wait_recv()
        total = self.near[0].astype(f32)
        for index in range(1, NEAR):
            total = total + self.near[index].astype(f32)
        self.part[...] = total.astype(bf16)
        self.loop(FAR, lambda other: self.part, self.far.at[self.layer], 1, self.far_device)
        self.far[self.layer] = self.part[...]

    def spread_near(self):
        self.batch(self.far, FAR, 1).wait_recv()
        total = self.far[0].astype(f32)
        for index in range(1, FAR):
            total = total + self.far[index].astype(f32)
        self.near_out[...] = (total * self.scale).astype(bf16)
        self.loop(NEAR, lambda other: self.near_out, self.out.at[self.mine], 2, self.near_device)
        self.out[self.mine] = self.near_out[...]

    def end(self):
        self.batch(self.out, NEAR, 2).wait_recv()
        self.batch(self.near, NEAR, 0).wait_send()
        self.batch(self.far, FAR, 1).wait_send()
        self.batch(self.out, NEAR, 2).wait_send()


def adder_scratch(rows):
    return [
        pltpu.VMEM((NEAR, rows, 128), bf16),
        pltpu.VMEM((NEAR, rows, 128), bf16),
        pltpu.VMEM((rows, 128), bf16),
        pltpu.VMEM((FAR, rows, 128), bf16),
        pltpu.VMEM((rows, 128), bf16),
    ]


def store_lanes(ref, row, array):
    height, block = array.shape[0], ref.shape[1]
    for index in range(array.shape[1] // 128):
        part = array[:, 128 * index : 128 * index + 128].astype(ref.dtype)
        start, done = row + height * index, 0
        while done < height:
            count = min(height - done, block - (start + done) % block)
            inside = (start + done) % block
            ref[(start + done) // block, inside : inside + count, :] = part[done : done + count]
            done += count


def load_lanes(ref, row, height, count):
    parts = [ref[row + height * index : row + height * (index + 1), :].astype(f32) for index in range(count)]
    return jnp.concatenate(parts, axis=1) if count > 1 else parts[0]


def main_kernel(
    scale,
    feats_ref, first_ref, ident_ref, second_ref, cotangent_ref,
    inlet_one, outlet_one, widen_one, narrow_one_t, pool_ref, inlet_two, outlet_two, widen_two, narrow_two,
    second_out, feats_out, sums_one, sums_two,
    mark, marks_in, send_one, rows_one, send_two, rows_two, send_three, rows_three, send_four, rows_four,
    places_ref, hits_ref, member_ref, taking_ref, inputs_ref, mixed_ref, attended_ref, shares_ref, hidden_ref,
    values_ref, slope_ref, normed_ref, norm_two_ref, rates_ref, powers_one, powers_two, *rest,
):
    me = lax.axis_index("pts")
    sems = rest[-1]
    late = Adder(scale, *rest[:5], sums_one, sems, 10)
    early = Adder(scale, *rest[5:10], sums_two, sems, 16)
    barrier = greet_peers(me)

    def greet_near(step, carry):
        pl.semaphore_signal(barrier, device_id=early.near_device(step)[1], device_id_type=MESH)
        return carry

    lax.fori_loop(1, NEAR, greet_near, 0)

    first, second = first_ref[...], second_ref[...]
    owner_one, owner_two = first // ROWS, second // COARSE
    rank_one, rank_two = ranks(owner_one), ranks(owner_two)
    slot_one, layer_one = owner_one * 16 + rank_one % 16, rank_one // 16
    feats = feats_ref[...].astype(f32)
    wide = [jnp.where(layer_one == index, feats, 0.0) for index in range(4)]
    wide = jnp.concatenate(wide, axis=0).astype(bf16)
    found = marks(owner_one, rank_one, first % ROWS + 1)
    found += marks(owner_two, rank_two + 64, second % COARSE + 1)
    mark[:, 0, :] = found
    pl.semaphore_wait(barrier, PEERS + NEAR - 2)
    marked = exchange(me, mark, marks_in, sems, 0)

    def pack(quarter):
        return dot_nt(match(slot_one - 256 * quarter, 256), wide).astype(bf16).reshape(16, 16, 256)

    moved_one = exchange_parts(me, pack, lambda: None, send_one, rows_one, sems, 2)

    taking_ref[...] = match(owner_two * 16 + rank_two, 1024)
    for patch in range(PATCHES):
        member_ref[patch] = match(ident_ref[:, patch * PATCH : (patch + 1) * PATCH], COARSE)
    weights_one = [inlet_one[...], outlet_one[...], widen_one[...], turned(narrow_one_t[...])]
    turned_one = [turned(weight) for weight in weights_one[:3]] + [narrow_one_t[...]]
    marked.wait_recv()
    places, drops = spread_places(marks_in[:, 0, :])
    for part in range(5):
        places_ref[part : part + 1, :] = places[part]
    kept = [jnp.where(drop, -1, place) for place, drop in zip(places, drops)]
    for layer in range(4):
        hits_ref[layer] = match(places[layer] % 512, 512)
    hits = [hits_ref[layer] for layer in range(4)]
    last = last_senders([[place // 512 == patch for patch in range(PATCHES)] for place in kept[:4]], hits)
    last_two = last_senders([[kept[4] >= 0]], [match(kept[4], COARSE)])
    places_ref[5:6, :] = jnp.where(last_two[0], kept[4], -1)
    moved_one.wait_recv()
    arrived = rows_one[...].reshape(1024, 256).astype(f32).T
    landed = jnp.zeros((256, 512), f32)
    for layer in range(4):
        place = jnp.where(last[layer], kept[layer], -1)
        points = arrived[64 * layer : 64 * layer + 64]
        spread = [jnp.where(place // 512 == patch, points, 0.0) for patch in range(PATCHES)]
        landed += dot_nt(jnp.concatenate(spread, axis=0).astype(bf16), hits[layer])
    inputs_ref[...] = landed.astype(bf16).reshape(PATCHES, 64, PATCH)
    total = jnp.zeros((80, COARSE), f32)
    for patch in range(PATCHES):
        result, mixed, attended, shares, hidden, values = block_front(
            inputs_ref[patch], *turned_one, powers_one, 4 * patch
        )
        mixed_ref[patch] = mixed
        attended_ref[patch] = attended
        shares_ref[patch] = shares
        hidden_ref[patch] = hidden
        values_ref[patch] = values.astype(bf16)
        counted = jnp.concatenate([result, jnp.ones((16, PATCH), bf16)], axis=0)
        total += dot_nt(counted, member_ref[patch])
    sizes = total[64:65]
    pooled = (total[:64] / sizes).astype(bf16)
    coarse = dot(turned(pool_ref[...]), pooled).astype(bf16)
    send_two[...] = dot_nt(taking_ref[...], coarse).astype(bf16).reshape(PEERS, 16, 128)
    moved_two = exchange(me, send_two, rows_two, sems, 4)

    def slopes(patch, carry):
        slope_ref[patch] = gelu_slope(values_ref[patch].astype(f32))
        return carry

    lax.fori_loop(0, PATCHES, slopes, 0)
    weights_two = [inlet_two[...], outlet_two[...], widen_two[...], narrow_two[...]]
    turned_two = [turned(weight) for weight in weights_two]
    gradient = turned(cotangent_ref[...])
    landing, taking_two = match(places_ref[5:6, :], COARSE), match(places_ref[4:5, :], COARSE)
    for patch in range(PATCHES):
        normed, rate, second, rate_two = norms(inputs_ref[patch], attended_ref[patch], turned_one[1])
        normed_ref[patch] = normed
        norm_two_ref[patch] = second
        rates_ref[patch] = jnp.concatenate([rate, rate_two], axis=0)
    moved_two.wait_recv()

    inputs = dot_nt(turned(rows_two[...].reshape(1024, 128)), landing).astype(bf16)
    result, mixed, attended, shares, hidden, values = block_front(inputs, *turned_two, powers_two, 0)
    back, grads_of = block_back(
        norms(inputs, attended, turned_two[1]), mixed, attended, shares, hidden, gelu_slope(values), gradient,
        weights_two, powers_two, 0,
    )
    send_three[...] = turned(dot(back, taking_two)).reshape(PEERS, 16, 128)
    moved_three = exchange(me, send_three, rows_three, sems, 6)
    row = 0
    for grad in grads_of():
        store_lanes(early.half, row, grad)
        row += grad.shape[0] * grad.shape[1] // 128
    second_out[...] = turned(result)
    moved_three.wait_recv()
    early.send_near()

    grad_coarse = dot(turned(rows_three[...].reshape(1024, 128)), taking_ref[...]).astype(bf16)
    grad_pool = dot_nt(pooled, grad_coarse)
    grad_pooled = dot(pool_ref[...], grad_coarse).astype(bf16).astype(f32)
    share = (grad_pooled / sizes).astype(bf16)

    backs, front_total, widen_total, narrow_total = [], 0.0, 0.0, 0.0
    for patch in range(PATCHES):
        gradient = dot(share, member_ref[patch]).astype(bf16)
        prepared = normed_ref[patch], rates_ref[patch, 0:1], norm_two_ref[patch], rates_ref[patch, 1:2]
        back, grads_of = block_back(
            prepared, mixed_ref[patch], attended_ref[patch], shares_ref[patch], hidden_ref[patch],
            slope_ref[patch], gradient, weights_one, powers_one, 4 * patch,
        )
        backs.append(back)
        grad_inlet, grad_outlet, grad_widen, grad_narrow = grads_of()
        front_total += jnp.concatenate([grad_inlet, grad_outlet], axis=1)
        widen_total += grad_widen
        narrow_total += grad_narrow
        if patch == 2:
            early.send_far()
    store_lanes(late.half, 0, front_total)
    store_lanes(late.half, 128, widen_total)
    store_lanes(late.half, 256, narrow_total)
    store_lanes(late.half, 384, grad_pool)
    late.half[28:] = jnp.zeros((4, 16, 128), bf16)
    late.send_near()
    back = jnp.concatenate(backs, axis=0)

    def take(quarter):
        taken = []
        for layer in range(4):
            place = places_ref[layer : layer + 1, pl.ds(pl.multiple_of(quarter * 256, 256), 256)]
            found = dot(back, hits_ref[layer, :, pl.ds(pl.multiple_of(quarter * 256, 256), 256)])
            parts = [
                jnp.where(place // 512 == patch, found[64 * patch : 64 * patch + 64], 0.0) for patch in range(PATCHES)
            ]
            taken.append(parts[0] + parts[1] + parts[2] + parts[3])
        return jnp.concatenate(taken, axis=0).T.astype(bf16).reshape(16, 16, 256)

    moved_four = exchange_parts(me, take, late.send_far, send_four, rows_four, sems, 8)
    picking = match(slot_one, 1024)
    early.spread_near()
    late.spread_near()
    moved_four.wait_recv()
    found = dot(turned(rows_four[...].reshape(1024, 256)), picking)
    parts = [jnp.where(layer_one == index, found[64 * index : 64 * index + 64], 0.0) for index in range(4)]
    feats_out[...] = (parts[0] + parts[1] + parts[2] + parts[3]).astype(bf16)
    early.end()
    late.end()
    marked.wait_send()
    moved_one.wait_send()
    moved_two.wait_send()
    moved_three.wait_send()
    moved_four.wait_send()


def output_kernel(
    second_in, feats_in, late_ref, early_ref,
    second_out, feats_out, inlet_one, outlet_one, widen_one, narrow_one_t, pool,
    inlet_two, outlet_two, widen_two, narrow_two,
):
    second_out[...] = second_in[...]
    feats_out[...] = feats_in[...]
    front = load_lanes(late_ref, 0, 64, 2)
    inlet_one[...] = front[:, :192]
    outlet_one[...] = front[:, 192:]
    widen_one[...] = load_lanes(late_ref, 128, 64, 2)
    narrow_one_t[...] = load_lanes(late_ref, 256, 64, 2)
    pool[...] = load_lanes(late_ref, 384, 64, 1)
    inlet_two[...] = load_lanes(early_ref, 0, 128, 3)
    outlet_two[...] = load_lanes(early_ref, 384, 128, 1)
    widen_two[...] = load_lanes(early_ref, 512, 128, 4)
    narrow_two[...] = load_lanes(early_ref, 1024, 128, 4).T


def call(kernel, outs, scratch, *operands, collective=None):
    params = {} if collective is None else {"collective_id": collective, "has_side_effects": True}
    whole = pl.BlockSpec(memory_space=pltpu.VMEM)
    return pl.pallas_call(
        kernel,
        out_shape=[jax.ShapeDtypeStruct(shape, dtype) for shape, dtype in outs],
        in_specs=[whole] * len(operands),
        out_specs=[whole] * len(outs),
        scratch_shapes=scratch,
        compiler_params=pltpu.CompilerParams(vmem_limit_bytes=56 * 2**20, **params),
    )(*operands)


def shards(
    feats,
    dest_first,
    pool_ids,
    dest_second,
    cotangent,
    inlet_first,
    outlet_first,
    widen_first,
    narrow_first,
    pool_weight,
    inlet_second,
    outlet_second,
    widen_second,
    narrow_second,
):
    scale = 1.0 / math.sqrt(lax.axis_size("rep") * lax.axis_size("pts") * COARSE)
    wide_slots, slots = pltpu.VMEM((PEERS, 16, 256), bf16), pltpu.VMEM((PEERS, 16, 128), bf16)
    mark = pltpu.VMEM((PEERS, 1, 128), f32)
    moved = call(
        lambda *refs: main_kernel(scale, *refs),
        [((COARSE, 128), bf16), ((64, ROWS), bf16), ((NEAR, 16, 128), bf16), ((NEAR, 48, 128), bf16)],
        [mark, mark, wide_slots, wide_slots, slots, slots, slots, slots, wide_slots, wide_slots]
        + [
            pltpu.VMEM((6, 1024), i32),
            pltpu.VMEM((4, 512, 1024), bf16),
            pltpu.VMEM((PATCHES, COARSE, PATCH), bf16),
            pltpu.VMEM((1024, COARSE), bf16),
            pltpu.VMEM((PATCHES, 64, PATCH), bf16),
            pltpu.VMEM((PATCHES, 192, PATCH), bf16),
            pltpu.VMEM((PATCHES, 64, PATCH), bf16),
            pltpu.VMEM((PATCHES, 4, PATCH), f32),
            pltpu.VMEM((PATCHES, 256, PATCH), bf16),
            pltpu.VMEM((PATCHES, 256, PATCH), bf16),
            pltpu.VMEM((PATCHES, 256, PATCH), bf16),
            pltpu.VMEM((PATCHES, 64, PATCH), f32),
            pltpu.VMEM((PATCHES, 64, PATCH), f32),
            pltpu.VMEM((PATCHES, 2, PATCH), f32),
            pltpu.VMEM((16, PATCH, PATCH), bf16),
            pltpu.VMEM((8, PATCH, PATCH), bf16),
        ]
        + adder_scratch(16)
        + adder_scratch(48)
        + [pltpu.SemaphoreType.DMA((22,))],
        feats[0].T, dest_first, pool_ids, dest_second, cotangent[0],
        inlet_first, outlet_first, widen_first, narrow_first.T, pool_weight,
        inlet_second, outlet_second, widen_second, narrow_second,
        collective=1,
    )
    second_out, feats_grad, late, early = moved
    weights = (inlet_first, outlet_first, widen_first, narrow_first.T, pool_weight)
    weights += (inlet_second, outlet_second, widen_second, narrow_second)
    second_out, feats_grad, *totals = call(
        output_kernel,
        [((COARSE, 128), bf16), ((64, ROWS), bf16)] + [(weight.shape, f32) for weight in weights],
        [],
        second_out, feats_grad, late.reshape(512, 128), early.reshape(1536, 128),
    )
    totals[3] = totals[3].T
    return (second_out[None], feats_grad.T[None], *totals)


def solution(mesh):
    split = P("rep", "pts")
    return jax.shard_map(
        shards,
        mesh=mesh,
        in_specs=(split,) * 5 + (P(),) * 9,
        out_specs=(split,) * 2 + (P(),) * 9,
        check_vma=False,
    )
```

```python
import math

import jax
import jax.numpy as jnp
from jax import lax
from jax.experimental import pallas as pl
from jax.experimental.pallas import tpu as pltpu
from jax.sharding import PartitionSpec as P


HEAD = 16
PATCH = 512
PATCHES = 4
ROWS = 2048
COARSE = 512
PEERS = 64
NEAR, FAR = 32, 8
MESH = pl.DeviceIdType.MESH
SHARPEN = HEAD**-0.5 / math.log(2.0)
f32, bf16, i32 = jnp.float32, jnp.bfloat16, jnp.int32


def dot(left, right):
    return jnp.dot(left, right, preferred_element_type=f32)


def dot_nt(left, right):
    return lax.dot_general(left, right, (((1,), (1,)), ((), ())), preferred_element_type=f32)


def turned(array):
    return array.astype(f32).T.astype(bf16)


def rows_of(count, width):
    return lax.broadcasted_iota(i32, (count, width), 0)


def match(row, count):
    return jnp.where(rows_of(count, row.shape[1]) == row, 1.0, 0.0).astype(bf16)


def norm(values):
    centred = values - jnp.mean(values, axis=0, keepdims=True)
    rate = lax.rsqrt(jnp.mean(centred * centred, axis=0, keepdims=True) + 1e-05)
    return centred * rate, rate


def norm_back(gradient, normed, rate):
    mean = jnp.mean(gradient, axis=0, keepdims=True)
    along = jnp.mean(gradient * normed, axis=0, keepdims=True)
    return rate * (gradient - mean - normed * along)


def padded(rows, head, width):
    parts = [rows]
    if head > 0:
        parts.insert(0, jnp.zeros((HEAD * head, rows.shape[1]), rows.dtype))
    rest = width - HEAD * (head + 1)
    if rest > 0:
        parts.append(jnp.zeros((rest, rows.shape[1]), rows.dtype))
    return jnp.concatenate(parts, axis=0)


def only(array, head):
    return padded(array[HEAD * head : HEAD * (head + 1)], head, array.shape[0])


def attend(mixed, width, powers_ref, first_power):
    keys = turned(mixed[width : 2 * width])
    ones = jnp.ones((HEAD, PATCH), bf16)
    outs, shares = [], []
    later = dot(keys, only(mixed[:width], 0))
    for head in range(width // HEAD):
        scores = later
        if head + 1 < width // HEAD:
            later = dot(keys, only(mixed[:width], head + 1))
        top = jnp.max(scores, axis=0, keepdims=True)
        powers = jnp.exp2((scores - top) * SHARPEN).astype(bf16)
        powers_ref[first_power + head] = powers
        start = 2 * width + HEAD * head
        sums = dot(jnp.concatenate([mixed[start : start + HEAD], ones], axis=0), powers)
        share = 1.0 / sums[HEAD : HEAD + 1]
        outs.append(sums[:HEAD] * share)
        shares.append(share)
    return jnp.concatenate(outs, axis=0).astype(bf16), jnp.concatenate(shares, axis=0)


def attend_back(mixed, attended, gradient, shares, width, powers_ref, first_power):
    keys = turned(mixed[width : 2 * width])
    values = turned(mixed[2 * width :])
    grad_queries, grad_keys, grad_values = [], [], []
    for group in range(0, width // HEAD, 4):
        spreads = []
        for head in range(group, group + 4):
            part = slice(HEAD * head, HEAD * (head + 1))
            shared = gradient[part] * shares[head : head + 1]
            overlap = jnp.sum(shared * attended[part].astype(f32), axis=0, keepdims=True)
            shared = shared.astype(bf16)
            spreads.append((dot(values, padded(shared, head, width)), overlap))
            grad_values.append(dot_nt(shared, powers_ref[first_power + head]))
        for head in range(group, group + 4):
            spread, overlap = spreads[head - group]
            powers = powers_ref[first_power + head].astype(f32)
            change = (powers * (spread - overlap)).astype(bf16)
            key_rows = mixed[width + HEAD * head : width + HEAD * (head + 1)]
            grad_queries.append(dot(key_rows, change) * HEAD**-0.5)
            grad_keys.append(dot_nt(mixed[HEAD * head : HEAD * (head + 1)], change) * HEAD**-0.5)
    return jnp.concatenate(grad_queries + grad_keys + grad_values, axis=0).astype(bf16)


def block_front(inputs, inlet_t, outlet_t, widen_t, narrow_t, powers_ref, first_power):
    width = inputs.shape[0]
    start = inputs.astype(f32)
    normed, rate = norm(start)
    mixed = dot(inlet_t, normed.astype(bf16)).astype(bf16)
    attended, shares = attend(mixed, width, powers_ref, first_power)
    middle = start + dot(outlet_t, attended)
    second, rate_two = norm(middle)
    values = dot(widen_t, second.astype(bf16))
    below = gelu_below(values)
    hidden = (values * below).astype(bf16)
    result = (middle + dot(narrow_t, hidden)).astype(bf16)
    return result, mixed, attended, shares, hidden, values, below, (normed, rate, second, rate_two)


def gelu_below(values):
    return 0.5 + 0.5 * lax.erf(values * math.sqrt(0.5))


def gelu_slope(values, below):
    bell = jnp.exp(-0.5 * values * values) * (1.0 / math.sqrt(2.0 * math.pi))
    return (below + values * bell).astype(bf16)


def norms(inputs, attended, outlet_t):
    start = inputs.astype(f32)
    return norm(start) + norm(start + dot(outlet_t, attended))


def block_back(prepared, mixed, attended, shares, hidden, slope, gradient, weights, powers_ref, first_power):
    inlet, outlet, widen, narrow = weights
    normed, rate, second, rate_two = prepared
    width = normed.shape[0]
    grad_wide = (dot(narrow, gradient) * slope.astype(f32)).astype(bf16)
    grad_middle = gradient.astype(f32) + norm_back(dot(widen, grad_wide), second, rate_two)
    short = grad_middle.astype(bf16)
    grad_mixed = attend_back(mixed, attended, dot(outlet, short), shares, width, powers_ref, first_power)
    grad_inputs = grad_middle + norm_back(dot(inlet, grad_mixed), normed, rate)

    def weight_grads():
        return (
            dot_nt(normed.astype(bf16), grad_mixed),
            dot_nt(attended, short),
            dot_nt(second.astype(bf16), grad_wide),
            dot_nt(gradient, hidden),
        )

    return grad_inputs.astype(bf16), weight_grads


def ranks(owner):
    before_me = jnp.where(rows_of(256, 256) < lax.broadcasted_iota(i32, (256, 256), 1), 1.0, 0.0)
    before_me = before_me.astype(bf16)
    before = jnp.zeros((PEERS, 1), f32)
    found = []
    for start in range(0, owner.shape[1], 256):
        hits = jnp.where(rows_of(PEERS, 256) == owner[:, start : start + 256], 1.0, 0.0)
        count = dot(hits.astype(bf16), before_me) + before
        found.append(jnp.sum(hits * count, axis=0, keepdims=True))
        before = before + jnp.sum(hits, axis=1, keepdims=True)
    return jnp.concatenate(found, axis=1).astype(i32)


def marks(owner, rank, value):
    hits = match(owner, PEERS)
    at = rows_of(128, owner.shape[1]) == rank
    high = jnp.where(at, (value >> 6).astype(f32), 0.0).astype(bf16)
    low = jnp.where(at, (value & 63).astype(f32), 0.0).astype(bf16)
    return dot_nt(hits, high) * 64.0 + dot_nt(hits, low)


def spread_places(table):
    lane = lax.broadcasted_iota(i32, (PEERS, 128), 1)
    apart = table + jnp.where(lane >= 64, 4096.0, 0.0)
    over = jnp.zeros((PEERS, 128), f32)
    for shift in range(1, 64):
        over = jnp.where(apart == pltpu.roll(apart, 128 - shift, 1), 1.0, over)
    high = jnp.floor(table * (1.0 / 64.0))
    low = table - 64.0 * high
    high = high + 64.0 * over
    stack = []
    for part in range(5):
        stack += [high[:, 16 * part : 16 * part + 16], low[:, 16 * part : 16 * part + 16]]
    stack = jnp.concatenate(stack, axis=0).astype(bf16)
    column = lax.broadcasted_iota(i32, (16, 1024), 1)
    spread = dot(stack, jnp.where(column % 16 == rows_of(16, 1024), 1.0, 0.0).astype(bf16))
    own = rows_of(PEERS, 1024) == lax.broadcasted_iota(i32, (PEERS, 1024), 1) // 16
    places, drops = [], []
    for part in range(5):
        high = jnp.sum(jnp.where(own, spread[128 * part : 128 * part + 64], 0.0), axis=0, keepdims=True)
        low = jnp.sum(jnp.where(own, spread[128 * part + 64 : 128 * part + 128], 0.0), axis=0, keepdims=True)
        drops.append(high > 63.5)
        high = jnp.where(high > 63.5, high - 64.0, high)
        places.append((high * 64.0 + low).astype(i32) - 1)
    return places, drops


def last_senders(inside, hits):
    width = hits[0].shape[0]
    count = len(inside[0])
    sender = lax.broadcasted_iota(i32, (1, 1024), 1) // 16
    own = rows_of(PEERS, 1024) == sender
    seen = jnp.zeros((PEERS * count, width), f32)
    for masks, hit in zip(inside, hits):
        wide = [jnp.where(own & mask, 1.0, 0.0) for mask in masks]
        seen += dot_nt(jnp.concatenate(wide, axis=0).astype(bf16), hit)
    index = rows_of(PEERS, width).astype(f32)
    lasts = []
    for part in range(count):
        lasts.append(jnp.max(jnp.where(seen[PEERS * part : PEERS * part + PEERS] > 0.5, index, -1.0), axis=0, keepdims=True))
    lasts = jnp.concatenate(lasts + [jnp.zeros((16 - count, width), f32)], axis=0).astype(bf16)
    found = []
    for masks, hit in zip(inside, hits):
        got = dot(lasts, hit)
        mine = jnp.full((1, 1024), -1.0, f32)
        for part in range(count):
            mine = jnp.where(masks[part], got[part : part + 1], mine)
        found.append(mine == sender.astype(f32))
    return found


def greet_peers(me):
    barrier = pltpu.get_barrier_semaphore()

    def greet(step, carry):
        pl.semaphore_signal(
            barrier, device_id={"pts": (me + step) % PEERS}, device_id_type=MESH
        )
        return carry

    lax.fori_loop(1, PEERS, greet, 0)
    return barrier


def send_to(source, target, sems, index, device):
    return pltpu.make_async_remote_copy(
        source, target, sems.at[index], sems.at[index + 1], device_id=device, device_id_type=MESH
    )


def batch_of(me, target, count, sems, index):
    some = target.at[pl.ds(0, count - 1)]
    return send_to(some, some, sems, index, {"pts": me})


def exchange(me, source, target, sems, index):

    def send(step, carry):
        along, across = step // 8, step // 2 % 4
        z = (me // 8 + 4 + (along + 1) // 2 * (1 - along % 2 * 2)) % 8
        y = (me // 2 + 2 + (across + 1) // 2 * (1 - across % 2 * 2)) % 4
        other = z * 8 + y * 2 + (me + 1 + step) % 2
        send_to(source.at[other], target.at[me], sems, index, {"pts": other}).start()
        return carry

    lax.fori_loop(0, PEERS - 1, send, 0)
    target[me] = source[me]
    return batch_of(me, target, PEERS, sems, index)


def exchange_parts(me, make_part, between, source, target, sems, index):
    for turn in (2, 1, 3, 0):
        quarter = (me // 16 + turn) % 4
        source[pl.ds(16 * quarter, 16)] = make_part(quarter)

        def send(step, carry, quarter=quarter):
            other = 16 * quarter + (me + step) % 16
            send_to(source.at[other], target.at[me], sems, index, {"pts": other}).start()
            return carry

        lax.fori_loop(1 if turn == 0 else 0, 16, send, 0)
        if turn == 1:
            between()
    target[me] = source[me]
    return batch_of(me, target, PEERS, sems, index)


class Adder:
    def __init__(self, scale, half, near, part, far, near_out, out, sems, index):
        self.scale, self.half, self.near, self.part, self.far = scale, half, near, part, far
        self.near_out, self.out, self.sems, self.index = near_out, out, sems, index
        self.me, rep = lax.axis_index("pts"), lax.axis_index("rep")
        self.inside, self.layer = self.me % 8, self.me // 8
        self.mine = self.inside * 4 + rep

    def near_device(self, step):
        other = (self.mine + step) % NEAR
        return other, {"pts": self.layer * 8 + other // 4, "rep": other % 4}

    def far_device(self, step):
        other = (self.layer + step) % FAR
        return other, {"pts": other * 8 + self.inside}

    def batch(self, target, count, stage):
        return batch_of(self.me, target, count, self.sems, self.index + 2 * stage)

    def loop(self, count, source_of, target, stage, device_of):
        def send(step, carry):
            other, device = device_of(step)
            send_to(source_of(other), target, self.sems, self.index + 2 * stage, device).start()
            return carry

        lax.fori_loop(1, count, send, 0)

    def send_near(self):
        self.loop(NEAR, lambda other: self.half.at[other], self.near.at[self.mine], 0, self.near_device)
        self.near[self.mine] = self.half[self.mine]

    def send_far(self):
        self.batch(self.near, NEAR, 0).wait_recv()
        total = self.near[0].astype(f32)
        for index in range(1, NEAR):
            total = total + self.near[index].astype(f32)
        self.part[...] = total.astype(bf16)
        self.loop(FAR, lambda other: self.part, self.far.at[self.layer], 1, self.far_device)
        self.far[self.layer] = self.part[...]

    def spread_near(self):
        self.batch(self.far, FAR, 1).wait_recv()
        total = self.far[0].astype(f32)
        for index in range(1, FAR):
            total = total + self.far[index].astype(f32)
        self.near_out[...] = (total * self.scale).astype(bf16)
        self.loop(NEAR, lambda other: self.near_out, self.out.at[self.mine], 2, self.near_device)
        self.out[self.mine] = self.near_out[...]

    def end(self):
        self.batch(self.out, NEAR, 2).wait_recv()
        self.batch(self.near, NEAR, 0).wait_send()
        self.batch(self.far, FAR, 1).wait_send()
        self.batch(self.out, NEAR, 2).wait_send()


def adder_scratch(rows):
    return [
        pltpu.VMEM((NEAR, rows, 128), bf16),
        pltpu.VMEM((NEAR, rows, 128), bf16),
        pltpu.VMEM((rows, 128), bf16),
        pltpu.VMEM((FAR, rows, 128), bf16),
        pltpu.VMEM((rows, 128), bf16),
    ]


def store_lanes(ref, row, array):
    height, block = array.shape[0], ref.shape[1]
    for index in range(array.shape[1] // 128):
        part = array[:, 128 * index : 128 * index + 128].astype(ref.dtype)
        start, done = row + height * index, 0
        while done < height:
            count = min(height - done, block - (start + done) % block)
            inside = (start + done) % block
            ref[(start + done) // block, inside : inside + count, :] = part[done : done + count]
            done += count


def load_lanes(ref, row, height, count):
    parts = [ref[row + height * index : row + height * (index + 1), :].astype(f32) for index in range(count)]
    return jnp.concatenate(parts, axis=1) if count > 1 else parts[0]


def main_kernel(
    scale,
    feats_ref, first_ref, ident_ref, second_ref, cotangent_ref,
    inlet_one, outlet_one, widen_one, narrow_one_t, pool_ref, inlet_two, outlet_two, widen_two, narrow_two,
    second_out, feats_out, sums_one, sums_two,
    mark, marks_in, send_one, rows_one, send_two, rows_two, send_three, rows_three, send_four, rows_four,
    places_ref, hits_ref, member_ref, taking_ref, inputs_ref, mixed_ref, attended_ref, shares_ref, hidden_ref,
    values_ref, slope_ref, normed_ref, norm_two_ref, rates_ref, powers_one, powers_two, *rest,
):
    me = lax.axis_index("pts")
    sems = rest[-1]
    late = Adder(scale, *rest[:5], sums_one, sems, 10)
    early = Adder(scale, *rest[5:10], sums_two, sems, 16)
    barrier = greet_peers(me)

    def greet_near(step, carry):
        pl.semaphore_signal(barrier, device_id=early.near_device(step)[1], device_id_type=MESH)
        return carry

    lax.fori_loop(1, NEAR, greet_near, 0)

    first, second = first_ref[...], second_ref[...]
    owner_one, owner_two = first // ROWS, second // COARSE
    rank_one, rank_two = ranks(owner_one), ranks(owner_two)
    slot_one, layer_one = owner_one * 16 + rank_one % 16, rank_one // 16
    feats = feats_ref[...].astype(f32)
    wide = [jnp.where(layer_one == index, feats, 0.0) for index in range(4)]
    wide = jnp.concatenate(wide, axis=0).astype(bf16)
    found = marks(owner_one, rank_one, first % ROWS + 1)
    found += marks(owner_two, rank_two + 64, second % COARSE + 1)
    mark[:, 0, :] = found
    pl.semaphore_wait(barrier, PEERS + NEAR - 2)
    marked = exchange(me, mark, marks_in, sems, 0)

    def pack(quarter):
        return dot_nt(match(slot_one - 256 * quarter, 256), wide).astype(bf16).reshape(16, 16, 256)

    moved_one = exchange_parts(me, pack, lambda: None, send_one, rows_one, sems, 2)

    taking_ref[...] = match(owner_two * 16 + rank_two, 1024)
    for patch in range(PATCHES):
        member_ref[patch] = match(ident_ref[:, patch * PATCH : (patch + 1) * PATCH], COARSE)
    weights_one = [inlet_one[...], outlet_one[...], widen_one[...], turned(narrow_one_t[...])]
    turned_one = [turned(weight) for weight in weights_one[:3]] + [narrow_one_t[...]]
    marked.wait_recv()
    places, drops = spread_places(marks_in[:, 0, :])
    for part in range(5):
        places_ref[part : part + 1, :] = places[part]
    kept = [jnp.where(drop, -1, place) for place, drop in zip(places, drops)]
    for layer in range(4):
        hits_ref[layer] = match(places[layer] % 512, 512)
    hits = [hits_ref[layer] for layer in range(4)]
    last = last_senders([[place // 512 == patch for patch in range(PATCHES)] for place in kept[:4]], hits)
    last_two = last_senders([[kept[4] >= 0]], [match(kept[4], COARSE)])
    places_ref[5:6, :] = jnp.where(last_two[0], kept[4], -1)
    moved_one.wait_recv()
    arrived = rows_one[...].reshape(1024, 256).astype(f32).T
    landed = jnp.zeros((256, 512), f32)
    for layer in range(4):
        place = jnp.where(last[layer], kept[layer], -1)
        points = arrived[64 * layer : 64 * layer + 64]
        spread = [jnp.where(place // 512 == patch, points, 0.0) for patch in range(PATCHES)]
        landed += dot_nt(jnp.concatenate(spread, axis=0).astype(bf16), hits[layer])
    inputs_ref[...] = landed.astype(bf16).reshape(PATCHES, 64, PATCH)
    total = jnp.zeros((80, COARSE), f32)
    for patch in range(PATCHES):
        result, mixed, attended, shares, hidden, values, *_ = block_front(
            inputs_ref[patch], *turned_one, powers_one, 4 * patch
        )
        mixed_ref[patch] = mixed
        attended_ref[patch] = attended
        shares_ref[patch] = shares
        hidden_ref[patch] = hidden
        values_ref[patch] = values.astype(bf16)
        counted = jnp.concatenate([result, jnp.ones((16, PATCH), bf16)], axis=0)
        total += dot_nt(counted, member_ref[patch])
    sizes = total[64:65]
    pooled = (total[:64] / sizes).astype(bf16)
    coarse = dot(turned(pool_ref[...]), pooled).astype(bf16)
    send_two[...] = dot_nt(taking_ref[...], coarse).astype(bf16).reshape(PEERS, 16, 128)
    moved_two = exchange(me, send_two, rows_two, sems, 4)

    def slopes(patch, carry):
        values = values_ref[patch].astype(f32)
        slope_ref[patch] = gelu_slope(values, gelu_below(values))
        return carry

    lax.fori_loop(0, PATCHES, slopes, 0)
    weights_two = [inlet_two[...], outlet_two[...], widen_two[...], narrow_two[...]]
    turned_two = [turned(weight) for weight in weights_two]
    gradient = turned(cotangent_ref[...])
    landing, taking_two = match(places_ref[5:6, :], COARSE), match(places_ref[4:5, :], COARSE)
    for patch in range(PATCHES):
        normed, rate, second, rate_two = norms(inputs_ref[patch], attended_ref[patch], turned_one[1])
        normed_ref[patch] = normed
        norm_two_ref[patch] = second
        rates_ref[patch] = jnp.concatenate([rate, rate_two], axis=0)
    moved_two.wait_recv()

    inputs = dot_nt(turned(rows_two[...].reshape(1024, 128)), landing).astype(bf16)
    result, mixed, attended, shares, hidden, values, below, prepared = block_front(inputs, *turned_two, powers_two, 0)
    back, grads_of = block_back(
        prepared, mixed, attended, shares, hidden, gelu_slope(values, below), gradient,
        weights_two, powers_two, 0,
    )
    send_three[...] = turned(dot(back, taking_two)).reshape(PEERS, 16, 128)
    moved_three = exchange(me, send_three, rows_three, sems, 6)
    row = 0
    for grad in grads_of():
        store_lanes(early.half, row, grad)
        row += grad.shape[0] * grad.shape[1] // 128
    second_out[...] = turned(result)
    moved_three.wait_recv()
    early.send_near()

    grad_coarse = dot(turned(rows_three[...].reshape(1024, 128)), taking_ref[...]).astype(bf16)
    grad_pool = dot_nt(pooled, grad_coarse)
    grad_pooled = dot(pool_ref[...], grad_coarse).astype(bf16).astype(f32)
    share = (grad_pooled / sizes).astype(bf16)

    backs, front_total, widen_total, narrow_total = [], 0.0, 0.0, 0.0
    for patch in range(PATCHES):
        gradient = dot(share, member_ref[patch]).astype(bf16)
        prepared = normed_ref[patch], rates_ref[patch, 0:1], norm_two_ref[patch], rates_ref[patch, 1:2]
        back, grads_of = block_back(
            prepared, mixed_ref[patch], attended_ref[patch], shares_ref[patch], hidden_ref[patch],
            slope_ref[patch], gradient, weights_one, powers_one, 4 * patch,
        )
        backs.append(back)
        grad_inlet, grad_outlet, grad_widen, grad_narrow = grads_of()
        front_total += jnp.concatenate([grad_inlet, grad_outlet], axis=1)
        widen_total += grad_widen
        narrow_total += grad_narrow
        if patch == 2:
            early.send_far()
    store_lanes(late.half, 0, front_total)
    store_lanes(late.half, 128, widen_total)
    store_lanes(late.half, 256, narrow_total)
    store_lanes(late.half, 384, grad_pool)
    late.half[28:] = jnp.zeros((4, 16, 128), bf16)
    late.send_near()
    back = jnp.concatenate(backs, axis=0)

    def take(quarter):
        taken = []
        for layer in range(4):
            place = places_ref[layer : layer + 1, pl.ds(pl.multiple_of(quarter * 256, 256), 256)]
            found = dot(back, hits_ref[layer, :, pl.ds(pl.multiple_of(quarter * 256, 256), 256)])
            parts = [
                jnp.where(place // 512 == patch, found[64 * patch : 64 * patch + 64], 0.0) for patch in range(PATCHES)
            ]
            taken.append(parts[0] + parts[1] + parts[2] + parts[3])
        return jnp.concatenate(taken, axis=0).T.astype(bf16).reshape(16, 16, 256)

    moved_four = exchange_parts(me, take, late.send_far, send_four, rows_four, sems, 8)
    picking = match(slot_one, 1024)
    early.spread_near()
    late.spread_near()
    moved_four.wait_recv()
    found = dot(turned(rows_four[...].reshape(1024, 256)), picking)
    parts = [jnp.where(layer_one == index, found[64 * index : 64 * index + 64], 0.0) for index in range(4)]
    feats_out[...] = (parts[0] + parts[1] + parts[2] + parts[3]).astype(bf16)
    early.end()
    late.end()
    marked.wait_send()
    moved_one.wait_send()
    moved_two.wait_send()
    moved_three.wait_send()
    moved_four.wait_send()


def output_kernel(
    second_in, feats_in, late_ref, early_ref,
    second_out, feats_out, inlet_one, outlet_one, widen_one, narrow_one_t, pool,
    inlet_two, outlet_two, widen_two, narrow_two,
):
    second_out[...] = second_in[...]
    feats_out[...] = feats_in[...]
    front = load_lanes(late_ref, 0, 64, 2)
    inlet_one[...] = front[:, :192]
    outlet_one[...] = front[:, 192:]
    widen_one[...] = load_lanes(late_ref, 128, 64, 2)
    narrow_one_t[...] = load_lanes(late_ref, 256, 64, 2)
    pool[...] = load_lanes(late_ref, 384, 64, 1)
    inlet_two[...] = load_lanes(early_ref, 0, 128, 3)
    outlet_two[...] = load_lanes(early_ref, 384, 128, 1)
    widen_two[...] = load_lanes(early_ref, 512, 128, 4)
    narrow_two[...] = load_lanes(early_ref, 1024, 128, 4).T


def call(kernel, outs, scratch, *operands, collective=None):
    params = {} if collective is None else {"collective_id": collective, "has_side_effects": True}
    whole = pl.BlockSpec(memory_space=pltpu.VMEM)
    return pl.pallas_call(
        kernel,
        out_shape=[jax.ShapeDtypeStruct(shape, dtype) for shape, dtype in outs],
        in_specs=[whole] * len(operands),
        out_specs=[whole] * len(outs),
        scratch_shapes=scratch,
        compiler_params=pltpu.CompilerParams(vmem_limit_bytes=56 * 2**20, **params),
    )(*operands)


def shards(
    feats,
    dest_first,
    pool_ids,
    dest_second,
    cotangent,
    inlet_first,
    outlet_first,
    widen_first,
    narrow_first,
    pool_weight,
    inlet_second,
    outlet_second,
    widen_second,
    narrow_second,
):
    scale = 1.0 / math.sqrt(lax.axis_size("rep") * lax.axis_size("pts") * COARSE)
    wide_slots, slots = pltpu.VMEM((PEERS, 16, 256), bf16), pltpu.VMEM((PEERS, 16, 128), bf16)
    mark = pltpu.VMEM((PEERS, 1, 128), f32)
    moved = call(
        lambda *refs: main_kernel(scale, *refs),
        [((COARSE, 128), bf16), ((64, ROWS), bf16), ((NEAR, 16, 128), bf16), ((NEAR, 48, 128), bf16)],
        [mark, mark, wide_slots, wide_slots, slots, slots, slots, slots, wide_slots, wide_slots]
        + [
            pltpu.VMEM((6, 1024), i32),
            pltpu.VMEM((4, 512, 1024), bf16),
            pltpu.VMEM((PATCHES, COARSE, PATCH), bf16),
            pltpu.VMEM((1024, COARSE), bf16),
            pltpu.VMEM((PATCHES, 64, PATCH), bf16),
            pltpu.VMEM((PATCHES, 192, PATCH), bf16),
            pltpu.VMEM((PATCHES, 64, PATCH), bf16),
            pltpu.VMEM((PATCHES, 4, PATCH), f32),
            pltpu.VMEM((PATCHES, 256, PATCH), bf16),
            pltpu.VMEM((PATCHES, 256, PATCH), bf16),
            pltpu.VMEM((PATCHES, 256, PATCH), bf16),
            pltpu.VMEM((PATCHES, 64, PATCH), f32),
            pltpu.VMEM((PATCHES, 64, PATCH), f32),
            pltpu.VMEM((PATCHES, 2, PATCH), f32),
            pltpu.VMEM((16, PATCH, PATCH), bf16),
            pltpu.VMEM((8, PATCH, PATCH), bf16),
        ]
        + adder_scratch(16)
        + adder_scratch(48)
        + [pltpu.SemaphoreType.DMA((22,))],
        feats[0].T, dest_first, pool_ids, dest_second, cotangent[0],
        inlet_first, outlet_first, widen_first, narrow_first.T, pool_weight,
        inlet_second, outlet_second, widen_second, narrow_second,
        collective=1,
    )
    second_out, feats_grad, late, early = moved
    weights = (inlet_first, outlet_first, widen_first, narrow_first.T, pool_weight)
    weights += (inlet_second, outlet_second, widen_second, narrow_second)
    second_out, feats_grad, *totals = call(
        output_kernel,
        [((COARSE, 128), bf16), ((64, ROWS), bf16)] + [(weight.shape, f32) for weight in weights],
        [],
        second_out, feats_grad, late.reshape(512, 128), early.reshape(1536, 128),
    )
    totals[3] = totals[3].T
    return (second_out[None], feats_grad.T[None], *totals)


def solution(mesh):
    split = P("rep", "pts")
    return jax.shard_map(
        shards,
        mesh=mesh,
        in_specs=(split,) * 5 + (P(),) * 9,
        out_specs=(split,) * 2 + (P(),) * 9,
        check_vma=False,
    )
```
